32 devices in a mesh: depth: 4 (over x, core), tile: 8 (over z, y).
Axes of the slice: x: 2, y: 2, z: 4, core: 2. Of those that a mesh axis runs over, the one named last changes fastest.
Arguments:
- velocity: float32 [3, 64, 256, 2048], P(None, 'depth', 'tile'), may hold values from -6 to 6
- view_sign: int32 [8], P('tile'), may hold values from 0 to 1, as said below
- brick_flags: int32 [8, 64, 16], P('depth', 'tile'), may hold values from 0 to 1, as said below
Outputs:
- image_color: float32 [3, 256, 2048], P(None, 'tile', 'depth')
- image_alpha: float32 [256, 2048], P('tile', 'depth')
The draws below stay inside these ranges and needn't reach their ends.
Inputs may be any that keep to these rules, and one draw needn't show every extreme that they name: `view_sign`: 0 views a band of 32 image rows from the first index along the first dimension, 1 from its last; exactly half of the bands hold 1. `brick_flags`: 1 marks a brick that is rendered, 0 a brick that is treated as empty.
All inputs are finite; a program needn't handle non-finite values.
Results may differ from the reference program's by a relative error of at most 0.00005.
Values sent between devices are 32-bit elements; how exact they have to be, the bound alone decides.
No kernel may reach another device: no remote copies, remote signals or barrier semaphores. Data moves between devices by JAX's collectives and lax.ppermute only.
A program may use at most 192 MiB of HBM per device.

```python
import jax
import jax.numpy as jnp
from jax import lax

CY = 32
NZ = 2048
NX = 64
NY = 256


def draw_view_sign(key, part):
    band_count = NY // CY
    order = jax.random.permutation(key, band_count)
    return (order < band_count // 2).astype(jnp.int32)


def draw_brick_flags(key, part):
    rows_y = NY // 4
    grid_shape = (NX // 8, rows_y, NZ // 128)
    dice_rolls = jax.random.randint(key, grid_shape, 0, 100)
    centre = jnp.abs(2 * jnp.arange(rows_y) - rows_y + 1)
    threshold = 95 - centre * 80 // rows_y
    return (dice_rolls < threshold[None, :, None]).astype(jnp.int32)


def steps_of(rng, shape, pieces, least, high):
    loudness, own = 1.0, jax.random.fold_in(rng, 6)
    for axis_at, shards_of in pieces:
        steps = jnp.exp(jax.random.uniform(jax.random.fold_in(own, axis_at), (shards_of,), jnp.float32, least / len(pieces), high / len(pieces)))
        loudness = loudness * jnp.repeat(steps, shape[axis_at] // shards_of).reshape([-1 if axis == axis_at else 1 for axis in range(len(shape))])
    return loudness


def scatter_about(own_key, shape, width, most, pieces=(), dtype=jnp.bfloat16):
    entries = width * jax.random.normal(own_key, shape, jnp.float32)
    if pieces:
        entries = entries * steps_of(own_key, shape, pieces, -0.22, 0.18)
    return jnp.clip(entries, -most, most).astype(dtype)


def setup_inputs(seed: int = 0) -> dict:
    arg_keys = jax.random.split(jax.random.key(seed), 4)
    velocity = scatter_about(arg_keys[0], (3, NX, NY, NZ), 1.0, 6.0, ((1, 4), (2, 8)), jnp.float32)
    view_sign = draw_view_sign(jax.random.fold_in(arg_keys[3], 71), 0)
    brick_flags = draw_brick_flags(jax.random.fold_in(arg_keys[3], 71), 0)
    return {"velocity": velocity, "view_sign": view_sign, "brick_flags": brick_flags}


ALPHA_PEAK = 0.04


def stencil(volume, along_dim):
    widths = [(0, 0)] * volume.ndim
    widths[along_dim] = (2, 2)
    padded = jnp.pad(volume, widths)
    length = volume.shape[along_dim]
    shifted = [lax.slice_in_dim(padded, k, k + length, axis=along_dim) for k in range(5)]
    return (shifted[0] - 8.0 * shifted[1] + 8.0 * shifted[3] - shifted[4]) / 12.0


def blur(volume, along_dim):
    widths = [(0, 0)] * volume.ndim
    widths[along_dim] = (1, 1)
    padded = jnp.pad(volume, widths)
    length = volume.shape[along_dim]
    return 0.25 * lax.slice_in_dim(padded, 0, length, axis=along_dim) + 0.5 * lax.slice_in_dim(padded, 1, length + 1, axis=along_dim) + 0.25 * lax.slice_in_dim(padded, 2, length + 2, axis=along_dim)


def qcriterion(gradient):
    diagonal = gradient[0][0] * gradient[0][0] + gradient[1][1] * gradient[1][1] + gradient[2][2] * gradient[2][2]
    crossed = gradient[0][1] * gradient[1][0] + gradient[0][2] * gradient[2][0] + gradient[1][2] * gradient[2][1]
    return -0.5 * (diagonal + 2.0 * crossed)


def reference(velocity, view_sign, brick_flags):
    gradient = [[stencil(velocity[i], j) for j in range(3)] for i in range(3)]
    qfield = qcriterion(gradient)
    for along_dim in range(3):
        qfield = blur(qfield, along_dim)
    speed_sq = jnp.sum(velocity * velocity, axis=0)
    flag_cells = jnp.repeat(jnp.repeat(jnp.repeat(brick_flags, 8, 0), 4, 1), 128, 2).astype(jnp.float32)
    opacity = ALPHA_PEAK * jax.nn.sigmoid(2.0 * qfield) * flag_cells
    colour = jnp.stack([jax.nn.sigmoid(qfield), jax.nn.sigmoid(speed_sq - 3.0), jax.nn.sigmoid(-2.0 * qfield)]) * opacity[None]
    flipped_rows = jnp.repeat(view_sign, CY) == 1
    opacity = jnp.where(flipped_rows[None, :, None], opacity[::-1], opacity)
    colour = jnp.where(flipped_rows[None, None, :, None], colour[:, ::-1], colour)
    transmit = jnp.cumprod(1.0 - opacity, axis=0)
    before = jnp.concatenate([jnp.ones_like(transmit[:1]), transmit[:-1]], axis=0)
    image_color = jnp.sum(before[None] * colour, axis=1)
    image_alpha = 1.0 - transmit[-1]
    return image_color, image_alpha
```

```python
import jax
import jax.numpy as jnp
from jax import lax
from jax.experimental import pallas as pl
from jax.experimental.pallas import tpu as pltpu
from jax.sharding import PartitionSpec as P

ALPHA_PEAK = 0.04
LANES = 128
SUB = 8
HALF = SUB // 2
MIB = 1 << 20
F32 = jnp.float32
Q_SCALE = -0.5 / (12.0 * 12.0 * 64.0)


def struct(*shape):
    return jax.ShapeDtypeStruct(shape, F32)


def leading(*block):
    return pl.BlockSpec(block, lambda b, n=len(block): (b,) + (0,) * (n - 1))


def trailing(*block):
    return pl.BlockSpec(block, lambda b, n=len(block): (0,) * (n - 1) + (b,))


ANYWHERE = pl.BlockSpec(memory_space=pl.ANY)
SCALARS = pl.BlockSpec(memory_space=pltpu.SMEM)


def cost(cells, ops, size):
    return pl.CostEstimate(flops=cells * ops, bytes_accessed=size, transcendentals=0)


def diff(m2, m1, p1, p2):
    if m2 is not None and m1 is not None and p1 is not None and p2 is not None:
        return 8.0 * (p1 - m1) + (m2 - p2)
    total = None
    for value, weight in ((m2, 1.0), (m1, -8.0), (p1, 8.0), (p2, -1.0)):
        if value is not None:
            total = weight * value if total is None else total + weight * value
    return total


def gradients_body(vel, q, speed, qe, speed_e, qx, gx, gy, cells, sems):
    _, nx, ny, nz = vel.shape
    nb, nj = nz // LANES, ny // SUB
    b = pl.program_id(0)

    def chunk(k):
        at = pl.ds(pl.multiple_of(k * LANES, LANES), LANES)
        return pltpu.make_async_copy(
            vel.at[:, :, :, at], cells.at[:, k + 1, :, SUB : SUB + ny, :], sems.at[k]
        )

    @pl.when(b == 0)
    def _():
        def begin(k, carry):
            chunk(k).start()
            return carry

        lax.fori_loop(0, nb, begin, 0)
        zero = jnp.zeros((SUB, LANES), F32)

        def clear_rows(k, carry):
            for i in range(3):
                for x in range(nx):
                    cells[i, k + 1, x, 0:SUB, :] = zero
                    cells[i, k + 1, x, SUB + ny : ny + 2 * SUB, :] = zero
            return carry

        lax.fori_loop(0, nb, clear_rows, 0)
        for i in range(3):
            for x in range(nx):
                for j in range(nj):
                    cells[i, 0, x, SUB * (j + 1) : SUB * (j + 2), :] = zero
                    cells[i, nb + 1, x, SUB * (j + 1) : SUB * (j + 2), :] = zero
        chunk(0).wait()

    @pl.when(b + 1 < nb)
    def _():
        chunk(b + 1).wait()

    lane = lax.broadcasted_iota(jnp.int32, (SUB, LANES), 1)
    sub = lax.broadcasted_iota(jnp.int32, (SUB, LANES), 0)
    edges = {0: 0, 1: 1, nx - 2: 2, nx - 1: 3}
    for j in range(nj):
        row = SUB * (j + 1)

        def tile(i, x, block=0, shift=0, row=row):
            return cells[i, b + 1 + block, x, pl.ds(row + shift, SUB), :]

        window = {(i, x): tile(i, x) for i in range(3) for x in range(2)}
        for x in range(nx):
            if x + 2 < nx:
                for i in range(3):
                    window[i, x + 2] = tile(i, x + 2)
            g = []
            for i in range(3):
                mid = window[i, x]
                left, right = tile(i, x, -1), tile(i, x, 1)
                along_x = diff(*[window.get((i, x + k)) for k in (-2, -1, 1, 2)])
                along_y = diff(*[tile(i, x, 0, k) for k in (-2, -1, 1, 2)])
                along_z = diff(
                    pltpu.roll(jnp.where(lane >= LANES - 2, left, mid), 2, 1),
                    pltpu.roll(jnp.where(lane >= LANES - 1, left, mid), 1, 1),
                    pltpu.roll(jnp.where(lane < 1, right, mid), LANES - 1, 1),
                    pltpu.roll(jnp.where(lane < 2, right, mid), LANES - 2, 1),
                )
                g.append((along_x, along_y, along_z))
            diagonal = g[0][0] * g[0][0] + g[1][1] * g[1][1] + g[2][2] * g[2][2]
            crossed = g[0][1] * g[1][0] + g[0][2] * g[2][0] + g[1][2] * g[2][1]
            q_here = diagonal + (crossed + crossed)
            u, v, w = window[0, x], window[1, x], window[2, x]
            speed_here = jnp.tanh(0.5 * (u * u + v * v + w * w) - 1.5)
            rows = pl.ds(SUB * j, SUB)
            q[0, x, rows, :] = q_here
            speed[0, x, rows, :] = speed_here
            if x in edges:
                qx[0, edges[x], rows, :] = q_here
                for k in range(3):
                    gx[0, k, edges[x], rows, :] = g[0][k]
            if j in (0, nj - 1):
                for ref, value in (
                    (qe.at[0, x], q_here),
                    (speed_e.at[0, x], speed_here),
                    (gy.at[0, 0, x], g[1][1]),
                    (gy.at[0, 1, x], g[1][0]),
                    (gy.at[0, 2, x], g[1][2]),
                ):
                    ref[...] = value if j == 0 else jnp.where(sub < HALF, ref[...], value)


def gradients(vel):
    _, nx, ny, nz = vel.shape
    nb = nz // LANES
    shapes = [(nx, ny), (nx, ny), (nx, SUB), (nx, SUB), (4, ny), (3, 4, ny), (3, nx, SUB)]
    return pl.pallas_call(
        gradients_body,
        grid=(nb,),
        in_specs=[ANYWHERE],
        out_specs=[leading(1, *s, LANES) for s in shapes],
        out_shape=[struct(nb, *s, LANES) for s in shapes],
        scratch_shapes=[
            pltpu.VMEM((3, nb + 2, nx, ny + 2 * SUB, LANES), F32),
            pltpu.SemaphoreType.DMA((nb,)),
        ],
        compiler_params=pltpu.CompilerParams(vmem_limit_bytes=44 * MIB),
        cost_estimate=cost(nx * ny * nz, 70, 6 * 4 * nx * ny * nz),
        name="gradients",
    )(vel)


def depth_edges_body(qx, gx, lo, hi, qx_out, fix_out):
    ny = qx.shape[2]
    sub = lax.broadcasted_iota(jnp.int32, (SUB, LANES), 0)
    for e in range(4):
        side = lo if e < 2 else hi
        for j in range(ny // SUB):
            rows = pl.ds(SUB * j, SUB)
            d = [side[i, e % 2, rows, :] for i in range(3)]
            g = [gx[0, k, e, rows, :] for k in range(3)]
            square = (g[0] + g[0] + d[0]) * d[0]
            crossed = g[1] * d[1] + g[2] * d[2]
            change = square + (crossed + crossed)
            qx_out[0, e, rows, :] = qx[0, e, rows, :] + change
            if j == 0:
                first = (change, d[1])
            if j == ny // SUB - 1:
                for k, value in enumerate((change, d[1])):
                    fix_out[0, k, e] = jnp.where(sub < HALF, first[k], value)


def depth_edges(qx, gx, lo, hi):
    nb, _, ny, _ = qx.shape
    return pl.pallas_call(
        depth_edges_body,
        grid=(nb,),
        in_specs=[
            leading(1, 4, ny, LANES),
            leading(1, 3, 4, ny, LANES),
            trailing(3, 2, ny, LANES),
            trailing(3, 2, ny, LANES),
        ],
        out_specs=[leading(1, 4, ny, LANES), leading(1, 2, 4, SUB, LANES)],
        out_shape=[struct(nb, 4, ny, LANES), struct(nb, 2, 4, SUB, LANES)],
        cost_estimate=cost(nb * 4 * ny * LANES, 12, nb * 4 * ny * LANES * 4 * 8),
        name="depth_edges",
    )(qx, gx, lo, hi)


def tile_edges_body(qe, gy, fix, lo, hi, qe_out, halo):
    nx = qe.shape[1]
    edges = {0: 0, 1: 1, nx - 2: 2, nx - 1: 3}

    @pl.when(pl.program_id(0) == 0)
    def _():
        halo[...] = jnp.zeros_like(halo)

    halo[:, :, 0:2, :] = lo[...]
    halo[:, :, SUB - 2 : SUB, :] = hi[...]
    for x in range(nx):
        e = [halo[i, x] for i in range(3)]
        g = [gy[0, k, x] for k in range(3)]
        q = qe[0, x]
        if x in edges:
            q = q + fix[0, 0, edges[x]]
            g[1] = g[1] + fix[0, 1, edges[x]]
        square = (g[0] + g[0] + e[1]) * e[1]
        crossed = g[1] * e[0] + g[2] * e[2]
        qe_out[0, x] = q + square + (crossed + crossed)


def tile_edges(qe, gy, fix, lo, hi):
    nb, nx, _, _ = qe.shape
    return pl.pallas_call(
        tile_edges_body,
        grid=(nb,),
        in_specs=[
            leading(1, nx, SUB, LANES),
            leading(1, 3, nx, SUB, LANES),
            leading(1, 2, 4, SUB, LANES),
            trailing(3, nx, 2, LANES),
            trailing(3, nx, 2, LANES),
        ],
        out_specs=leading(1, nx, SUB, LANES),
        out_shape=struct(nb, nx, SUB, LANES),
        scratch_shapes=[pltpu.VMEM((3, nx, SUB, LANES), F32)],
        cost_estimate=cost(nb * nx * SUB * LANES, 14, nb * nx * SUB * LANES * 4 * 6),
        name="tile_edges",
    )(qe, gy, fix, lo, hi)


def render_body(bricks, rows_too, *refs):
    if rows_too:
        sign, flags, q, lo, hi, row_lo, row_hi, speed, out, cells, smooth, sems = refs
    else:
        sign, flags, q, qx, lo, hi, speed, out, cells, smooth, sems = refs
    nb, nx, ny, _ = q.shape
    nj = ny // SUB
    b = pl.program_id(0)

    def chunk(k):
        to = cells.at[k]
        rows = pl.ds(SUB, ny)
        if rows_too:
            pairs = [
                (q.at[k], to.at[pl.ds(1, nx), rows]),
                (row_lo.at[k], to.at[:, SUB - 1]),
                (row_hi.at[k], to.at[:, SUB + ny]),
            ]
        else:
            pairs = [
                (q.at[k, pl.ds(2, nx - 4)], to.at[pl.ds(3, nx - 4), rows]),
                (qx.at[k, pl.ds(0, 2)], to.at[pl.ds(1, 2), rows]),
                (qx.at[k, pl.ds(2, 2)], to.at[pl.ds(nx - 1, 2), rows]),
            ]
        pairs += [(lo.at[k], to.at[0, rows]), (hi.at[k], to.at[nx + 1, rows])]
        return [pltpu.make_async_copy(s, t, sems.at[k, n]) for n, (s, t) in enumerate(pairs)]

    @pl.when(b == 0)
    def _():
        def begin(k, carry):
            for copy in chunk(k):
                copy.start()
            return carry

        lax.fori_loop(0, nb, begin, 0)
        zero = jnp.zeros((SUB, LANES), F32)
        for x in range(nx):
            for j in range(nj):
                smooth[0, x, SUB * j : SUB * (j + 1), :] = zero
                smooth[nb + 1, x, SUB * j : SUB * (j + 1), :] = zero

    @pl.when(b < nb)
    def _():
        for copy in chunk(b):
            copy.wait()
        for j in range(nj):
            before = here = None
            for x in range(nx + 2):
                up, mid, down = [cells[b, x, pl.ds(SUB * (j + 1) + k, SUB), :] for k in (-1, 0, 1)]
                after = (up + down) + (mid + mid)
                if x >= 2:
                    smooth[b + 1, x - 2, SUB * j : SUB * (j + 1), :] = (before + after) + (here + here)
                before, here = here, after

    @pl.when(b > 0)
    def _():
        lane = lax.broadcasted_iota(jnp.int32, (SUB, LANES), 1)
        sub = lax.broadcasted_iota(jnp.int32, (SUB, LANES), 0)
        flipped = sign[0] == 1
        for j in range(nj):
            left_over = jnp.ones((SUB, LANES), F32)
            sums = [jnp.zeros((SUB, LANES), F32) for _ in range(3)]
            rows = pl.ds(SUB * j, SUB)
            for n in range(nx):
                x = jnp.where(flipped, nx - 1 - n, n)
                if n % 8 == 0:
                    upper, lower = [flags[x // 8, k, b - 1].astype(F32) for k in bricks[j]]
                    peak = (0.5 * ALPHA_PEAK) * jnp.where(sub < HALF, upper, lower)
                mid = smooth[b, x, rows, :]
                left = pltpu.roll(jnp.where(lane >= LANES - 1, smooth[b - 1, x, rows, :], mid), 1, 1)
                right = pltpu.roll(jnp.where(lane < 1, smooth[b + 1, x, rows, :], mid), LANES - 1, 1)
                total = (left + right) + (mid + mid)
                wide = jnp.tanh((0.5 * Q_SCALE) * total)
                steep = jnp.tanh(Q_SCALE * total)
                weight = left_over * (peak + peak * steep)
                left_over = left_over - weight
                sums[0] = sums[0] + weight * wide
                sums[1] = sums[1] + weight * speed[0, x, rows, :]
                sums[2] = sums[2] - weight * steep
            alpha = 1.0 - left_over
            for k in range(3):
                out[k, rows, :] = 0.5 * (alpha + sums[k])
            out[3, rows, :] = left_over


def render(sign, flags, q, fixed, rows, speed, bricks):
    nb, nx, ny, _ = q.shape
    return pl.pallas_call(
        lambda *refs: render_body(bricks, bool(rows), *refs),
        grid=(nb + 1,),
        in_specs=[SCALARS, SCALARS]
        + [ANYWHERE] * (1 + len(fixed) + len(rows))
        + [pl.BlockSpec((1, nx, ny, LANES), lambda b: (jnp.maximum(b - 1, 0), 0, 0, 0))],
        out_specs=pl.BlockSpec((4, ny, LANES), lambda b: (0, 0, jnp.maximum(b - 1, 0))),
        out_shape=struct(4, ny, nb * LANES),
        scratch_shapes=[
            pltpu.VMEM((nb, nx + 2, ny + 2 * SUB, LANES), F32),
            pltpu.VMEM((nb + 2, nx, ny, LANES), F32),
            pltpu.SemaphoreType.DMA((nb, 5)),
        ],
        compiler_params=pltpu.CompilerParams(vmem_limit_bytes=32 * MIB),
        cost_estimate=cost(nb * nx * ny * LANES, 30, nb * nx * ny * LANES * 4 * 2),
        name="render_edges" if rows else "render",
    )(sign, flags, q, *fixed, *rows, speed)


def shifted(value, axis, step):
    count = lax.axis_size(axis)
    return lax.ppermute(value, axis, [(i, i + step) for i in range(count) if 0 <= i + step < count])


def from_partner(value, axis, bit):
    mask = 2**bit
    pairs = [(source, source ^ mask) for source in range(lax.axis_size(axis))]
    return lax.ppermute(value, axis, pairs)


def composite(partial, flipped):
    _, ny, nz = partial.shape
    depth_count = lax.axis_size("depth")
    width = nz // depth_count
    position = lax.axis_index("depth")
    current = partial.reshape(4, ny, depth_count, width)
    for bit in range(depth_count.bit_length() - 1):
        view = current.reshape(4, ny, current.shape[2] // 2, 2, width)
        is_lower = position >> bit & 1 == 0
        keep = jnp.where(is_lower, view[:, :, :, 0], view[:, :, :, 1])
        give = jnp.where(is_lower, view[:, :, :, 1], view[:, :, :, 0])
        take = from_partner(give, "depth", bit)
        front = jnp.where(is_lower != flipped, keep, take)
        back = jnp.where(is_lower != flipped, take, keep)
        current = jnp.concatenate([front[:3], jnp.zeros_like(front[3:])]) + front[3:] * back
    return current.reshape(4, ny, width)


def per_device(vel, view_sign, brick_flags):
    _, nx, ny, nz = vel.shape
    nb = nz // LANES
    bricks = brick_flags.shape[1]
    first, second = vel[:, :, 0:1], vel[:, :, 1:2]
    fourth, third = vel[:, :, ny - 1 :], vel[:, :, ny - 2 : ny - 1]
    rows_lo = shifted(jnp.concatenate([third - 8.0 * fourth, fourth], axis=2), "tile", 1)
    rows_hi = shifted(jnp.concatenate([-first, 8.0 * first - second], axis=2), "tile", -1)
    first, second = vel[:, 0:1], vel[:, 1:2]
    fourth, third = vel[:, nx - 1 :], vel[:, nx - 2 : nx - 1]
    layers_lo = shifted(jnp.concatenate([third - 8.0 * fourth, fourth], axis=1), "depth", 1)
    layers_hi = shifted(jnp.concatenate([-first, 8.0 * first - second], axis=1), "depth", -1)

    q, speed, qe, speed_e, qx, gx, gy = gradients(vel)
    qx, fix = depth_edges(qx, gx, layers_lo, layers_hi)
    q_lo = shifted(qx[:, 3], "depth", 1)
    q_hi = shifted(qx[:, 0], "depth", -1)
    main = render(
        view_sign,
        brick_flags,
        q,
        (qx, q_lo, q_hi),
        (),
        speed,
        [(2 * j, 2 * j + 1) for j in range(ny // SUB)],
    )
    qe = tile_edges(qe, gy, fix, rows_lo, rows_hi)
    e_lo = shifted(qe[:, nx - 1], "depth", 1)
    e_hi = shifted(qe[:, 0], "depth", -1)
    last = jnp.concatenate([e_lo[:, None, SUB - 1], qe[:, :, SUB - 1], e_hi[:, None, SUB - 1]], axis=1)
    head = jnp.concatenate([e_lo[:, None, 0], qe[:, :, 0], e_hi[:, None, 0]], axis=1)
    row_lo = shifted(last, "tile", 1)
    row_hi = shifted(head, "tile", -1)
    side = render(
        view_sign, brick_flags, qe, (e_lo, e_hi), (row_lo, row_hi), speed_e, [(0, bricks - 1)]
    )
    partial = jnp.concatenate([side[:, 0:3], main[:, 3 : ny - 3], side[:, SUB - 3 :]], axis=1)
    image = composite(partial, view_sign[0] == 1)
    return image[:3], 1.0 - image[3]


def solution(mesh):
    placed = (P(None, "depth", "tile", None), P("tile"), P("depth", "tile", None))
    return jax.shard_map(
        per_device,
        mesh=mesh,
        in_specs=placed,
        out_specs=(P(None, "tile", "depth"), P("tile", "depth")),
        check_vma=False,
    )
```

```python
import jax
import jax.numpy as jnp
from jax import lax
from jax.experimental import pallas as pl
from jax.experimental.pallas import tpu as pltpu
from jax.sharding import PartitionSpec as P

ALPHA_PEAK = 0.04
LANES = 128
SUB = 8
HALF = SUB // 2
VMEM = 60 << 20
F32 = jnp.float32
Q_SCALE = -0.5 / (12.0 * 12.0 * 64.0)


def struct(*shape):
    return jax.ShapeDtypeStruct(shape, F32)


def leading(*block):
    return pl.BlockSpec(block, lambda b, n=len(block): (b,) + (0,) * (n - 1))


def steps_of(blocks):
    return 4 if blocks % 4 == 0 else 1


ANYWHERE = pl.BlockSpec(memory_space=pl.ANY)
WHOLE = pl.BlockSpec(memory_space=pltpu.VMEM)
SCALARS = pl.BlockSpec(memory_space=pltpu.SMEM)


def cost(microseconds):
    size = int(microseconds * 3e6)
    return pl.CostEstimate(flops=0, bytes_accessed=size, transcendentals=0)


def diff(m2, m1, p1, p2):
    if m2 is not None and m1 is not None and p1 is not None and p2 is not None:
        return 8.0 * (p1 - m1) + (m2 - p2)
    total = None
    for value, weight in ((m2, 1.0), (m1, -8.0), (p1, 8.0), (p2, -1.0)):
        if value is not None:
            total = weight * value if total is None else total + weight * value
    return total


def send_rows_body(vel, head, tail, sems):
    ny = vel.shape[2]
    nb = head.shape[0]

    def copies(k):
        at = pl.ds(pl.multiple_of(k * LANES, LANES), LANES)
        return [
            pltpu.make_async_copy(vel.at[:, :, pl.ds(row, 2), at], to.at[k], sems.at[n, k])
            for n, (row, to) in enumerate(((0, head), (ny - 2, tail)))
        ]

    run(copies, nb)


def send_layers_body(vel, head, tail, sems):
    nx = vel.shape[1]
    nb = head.shape[0]

    def copies(k):
        at = pl.ds(pl.multiple_of(k * LANES, LANES), LANES)
        return [
            pltpu.make_async_copy(vel.at[:, pl.ds(x, 2), :, at], to.at[k], sems.at[n, k])
            for n, (x, to) in enumerate(((0, head), (nx - 2, tail)))
        ]

    run(copies, nb)


def run(copies, count):
    def begin(k, carry):
        for copy in copies(k):
            copy.start()
        return carry

    def finish(k, carry):
        for copy in copies(k):
            copy.wait()
        return carry

    lax.fori_loop(0, count, begin, 0)
    lax.fori_loop(0, count, finish, 0)


def sends(body, vel, *block):
    nb = vel.shape[3] // LANES
    return pl.pallas_call(
        body,
        in_specs=[ANYWHERE],
        out_specs=[ANYWHERE] * 2,
        out_shape=[struct(nb, *block, LANES)] * 2,
        scratch_shapes=[pltpu.SemaphoreType.DMA((2, nb))],
        name=body.__name__,
    )(vel)


def volume_body(sign, flags, vel, mid, qi, qx, speed_x, gx, qe, speed_e, gy, cells, qring, smooth, sems):
    _, nx, ny, nz = vel.shape
    nb, nj = nz // LANES, ny // SUB
    b = pl.program_id(0)

    def chunk(k):
        at = pl.ds(pl.multiple_of(k * LANES, LANES), LANES)
        return pltpu.make_async_copy(
            vel.at[:, :, :, at], cells.at[:, k + 1, :, SUB : SUB + ny, :], sems.at[k]
        )

    @pl.when(b == 0)
    def _():
        def begin(k, carry):
            chunk(k).start()
            return carry

        lax.fori_loop(0, nb, begin, 0)
        zero = jnp.zeros((SUB, LANES), F32)

        def clear_rows(k, carry):
            for i in range(3):
                for x in range(nx):
                    cells[i, k + 1, x, 0:SUB, :] = zero
                    cells[i, k + 1, x, SUB + ny : ny + 2 * SUB, :] = zero
            return carry

        lax.fori_loop(0, nb, clear_rows, 0)
        for j in range(nj):
            for x in range(nx):
                for i in range(3):
                    cells[i, 0, x, SUB * (j + 1) : SUB * (j + 2), :] = zero
                    cells[i, nb + 1, x, SUB * (j + 1) : SUB * (j + 2), :] = zero
            for x in range(nx - 6):
                smooth[0, x, SUB * j : SUB * (j + 1), :] = zero
                smooth[nb + 1, x, SUB * j : SUB * (j + 1), :] = zero
        chunk(0).wait()

    @pl.when(b + 1 < nb)
    def _():
        chunk(b + 1).wait()

    lane = lax.broadcasted_iota(jnp.int32, (SUB, LANES), 1)
    sub = lax.broadcasted_iota(jnp.int32, (SUB, LANES), 0)
    outer = {0: 0, 1: 1, nx - 2: 2, nx - 1: 3}
    inner = {2: 0, 3: 1, nx - 4: 2, nx - 3: 3}
    ends = {0: 0, 1: 1, 2: 2, nx - 3: 3, nx - 2: 4, nx - 1: 5}

    def q_stage():
        for j in range(nj):
            row = SUB * (j + 1)

            def tile(i, x, block=0, shift=0, row=row):
                return cells[i, b + 1 + block, x, pl.ds(row + shift, SUB), :]

            window = {(i, x): tile(i, x) for i in range(3) for x in range(2)}
            for x in range(nx):
                if x + 2 < nx:
                    for i in range(3):
                        window[i, x + 2] = tile(i, x + 2)
                g = []
                for i in range(3):
                    here = window[i, x]
                    left, right = tile(i, x, -1), tile(i, x, 1)
                    along_x = diff(*[window.get((i, x + k)) for k in (-2, -1, 1, 2)])
                    along_y = diff(*[tile(i, x, 0, k) for k in (-2, -1, 1, 2)])
                    along_z = diff(
                        pltpu.roll(jnp.where(lane >= LANES - 2, left, here), 2, 1),
                        pltpu.roll(jnp.where(lane >= LANES - 1, left, here), 1, 1),
                        pltpu.roll(jnp.where(lane < 1, right, here), LANES - 1, 1),
                        pltpu.roll(jnp.where(lane < 2, right, here), LANES - 2, 1),
                    )
                    g.append((along_x, along_y, along_z))
                diagonal = g[0][0] * g[0][0] + g[1][1] * g[1][1] + g[2][2] * g[2][2]
                crossed = g[0][1] * g[1][0] + g[0][2] * g[2][0] + g[1][2] * g[2][1]
                q_here = diagonal + (crossed + crossed)
                rows = pl.ds(SUB * j, SUB)
                qring[b % 2, x, rows, :] = q_here
                if x in outer:
                    qx[0, outer[x], rows, :] = q_here
                    for k in range(3):
                        gx[0, k, outer[x], rows, :] = g[0][k]
                if x in inner:
                    qi[0, inner[x], rows, :] = q_here
                if x in ends or j in (0, nj - 1):
                    speed_here = speed_term([window[i, x] for i in range(3)])
                if x in ends:
                    speed_x[0, ends[x], rows, :] = speed_here
                if j in (0, nj - 1):
                    for ref, value in (
                        (qe.at[0, x], q_here),
                        (speed_e.at[0, x], speed_here),
                        (gy.at[0, 0, x], g[1][1]),
                        (gy.at[0, 1, x], g[1][0]),
                        (gy.at[0, 2, x], g[1][2]),
                    ):
                        ref[...] = value if j == 0 else jnp.where(sub < HALF, ref[...], value)
                yield

    def blur_stage():
        for start in inner_starts(ny):
            before = here = None
            for x in range(2, nx - 2):
                after = blurred_rows(qring.at[(b - 1) % 2, x], start)
                if x >= 4:
                    smooth[b, x - 4, pl.ds(start, SUB), :] = (before + after) + (here + here)
                before, here = here, after
                yield

    def light_stage():
        c = b - 3
        flipped = sign[0] == 1
        for j in range(nj):
            state = Light()
            rows = pl.ds(SUB * j, SUB)
            for n in range(3, nx - 3):
                x = jnp.where(flipped, nx - 1 - n, n)
                if n == 3 or n % 8 == 0:
                    peak = peaks(flags, x // 8, (2 * j, 2 * j + 1), c, sub)
                total = blurred_lanes(*[smooth[c + k, x - 3, rows, :] for k in range(3)], lane)
                speed = speed_term([cells[i, c + 1, x, pl.ds(SUB * (j + 1), SUB), :] for i in range(3)])
                state.add(total, speed, peak)
                yield
            for k, value in enumerate(state.sums + [state.left]):
                mid[k, rows, :] = value

    def together(stages):
        units = [[stage, count, 0] for stage, count in stages]
        steps = max(count for _, count in stages)
        for step in range(steps + 1):
            for unit in units:
                while unit[0] is not None and unit[2] * steps <= step * unit[1]:
                    unit[2] += 1
                    if next(unit[0], 0) == 0:
                        unit[0] = None

    q_units, blur_units, light_units = nj * nx, nj * (nx - 4), nj * (nx - 6)

    @pl.when(b < 3)
    def _():
        together([(q_stage(), q_units)])

    @pl.when(((b >= 1) & (b < 3)) | (b == nb))
    def _():
        together([(blur_stage(), blur_units)])

    @pl.when((b >= 3) & (b < nb))
    def _():
        together([(q_stage(), q_units), (blur_stage(), blur_units), (light_stage(), light_units)])

    @pl.when(b >= nb)
    def _():
        together([(light_stage(), light_units)])


def inner_starts(ny):
    return [1 + SUB * k for k in range(ny // SUB - 1)] + [ny - SUB - 1]


def blurred_rows(ref, start):
    up, mid, down = [ref[pl.ds(start + k, SUB), :] for k in (-1, 0, 1)]
    return (up + down) + (mid + mid)


def blurred_lanes(left, mid, right, lane):
    left = pltpu.roll(jnp.where(lane >= LANES - 1, left, mid), 1, 1)
    right = pltpu.roll(jnp.where(lane < 1, right, mid), LANES - 1, 1)
    return (left + right) + (mid + mid)


def speed_term(u):
    return jnp.tanh(0.5 * (u[0] * u[0] + u[1] * u[1] + u[2] * u[2]) - 1.5)


def peaks(flags, x, rows, column, sub):
    upper, lower = [flags[x, row, column].astype(F32) for row in rows]
    return (0.5 * ALPHA_PEAK) * jnp.where(sub < HALF, upper, lower)


class Light:
    def __init__(self):
        self.left = jnp.ones((SUB, LANES), F32)
        self.sums = [jnp.zeros((SUB, LANES), F32) for _ in range(3)]

    def add(self, total, speed, peak):
        steep = jnp.tanh(Q_SCALE * total)
        weight = self.left * (peak + peak * steep)
        self.left = self.left - weight
        terms = (jnp.tanh((0.5 * Q_SCALE) * total), speed, -steep)
        self.sums = [s + weight * t for s, t in zip(self.sums, terms)]

    def behind(self, sums, left):
        self.sums = [s + self.left * t for s, t in zip(self.sums, sums)]
        self.left = self.left * left


def volume(sign, flags, vel):
    _, nx, ny, nz = vel.shape
    nb = nz // LANES
    shapes = [(4, ny), (4, ny), (6, ny), (3, 4, ny), (nx, SUB), (nx, SUB), (3, nx, SUB)]

    def spec(s):
        block = (1, *s, LANES)
        return pl.BlockSpec(block, lambda b, n=len(block): (jnp.minimum(b, nb - 1),) + (0,) * (n - 1))

    return pl.pallas_call(
        volume_body,
        grid=(nb + 3,),
        in_specs=[SCALARS, SCALARS, ANYWHERE],
        out_specs=[pl.BlockSpec((4, ny, LANES), lambda b: (0, 0, jnp.clip(b - 3, 0, nb - 1)))]
        + [spec(s) for s in shapes],
        out_shape=[struct(4, ny, nz)] + [struct(nb, *s, LANES) for s in shapes],
        scratch_shapes=[
            pltpu.VMEM((3, nb + 2, nx, ny + 2 * SUB, LANES), F32),
            pltpu.VMEM((2, nx, ny, LANES), F32),
            pltpu.VMEM((nb + 2, nx - 6, ny, LANES), F32),
            pltpu.SemaphoreType.DMA((nb,)),
        ],
        compiler_params=pltpu.CompilerParams(vmem_limit_bytes=VMEM),
        cost_estimate=cost(20),
        name="volume",
    )(sign, flags, vel)


def depth_edges_body(qx, gx, lo, hi, qx_out, first_out, last_out, fix_out):
    count, _, ny, _ = qx.shape
    sub = lax.broadcasted_iota(jnp.int32, (SUB, LANES), 0)

    def block(k, carry):
        for e in range(4):
            for j in range(ny // SUB):
                rows = pl.ds(SUB * j, SUB)
                d = []
                for i in range(3):
                    near = [(lo if e < 2 else hi)[k, i, n, rows, :] for n in range(2)]
                    d.append((near[0] - 8.0 * near[1], near[1], -near[0], 8.0 * near[0] - near[1])[e])
                g = [gx[k, n, e, rows, :] for n in range(3)]
                square = (g[0] + g[0] + d[0]) * d[0]
                crossed = g[1] * d[1] + g[2] * d[2]
                change = square + (crossed + crossed)
                fixed = qx[k, e, rows, :] + change
                qx_out[k, e, rows, :] = fixed
                if e == 0:
                    first_out[k, rows, :] = fixed
                if e == 3:
                    last_out[k, rows, :] = fixed
                if j == 0:
                    first = (change, d[1])
                if j == ny // SUB - 1:
                    for n, value in enumerate((change, d[1])):
                        fix_out[k, n, e] = jnp.where(sub < HALF, first[n], value)
        return carry

    lax.fori_loop(0, count, block, 0)


def depth_edges(qx, gx, lo, hi):
    nb, _, ny, _ = qx.shape
    step = steps_of(nb)
    outs = [(4, ny), (ny,), (ny,), (2, 4, SUB)]
    return pl.pallas_call(
        depth_edges_body,
        grid=(nb // step,),
        in_specs=[
            leading(step, 4, ny, LANES),
            leading(step, 3, 4, ny, LANES),
            leading(step, 3, 2, ny, LANES),
            leading(step, 3, 2, ny, LANES),
        ],
        out_specs=[leading(step, *s, LANES) for s in outs],
        out_shape=[struct(nb, *s, LANES) for s in outs],
        compiler_params=pltpu.CompilerParams(vmem_limit_bytes=VMEM),
        cost_estimate=cost(3),
        name="depth_edges",
    )(qx, gx, lo, hi)


def tile_edges_body(qe, gy, fix, lo, hi, qe_out, first_out, last_out, head_out, tail_out, halo, sems):
    count, nx, _, _ = qe.shape
    nb = lo.shape[0]
    outer = {0: 0, 1: 1, nx - 2: 2, nx - 1: 3}
    step = pl.program_id(0)

    def copies(k):
        at = pl.ds(k * count, count)
        return [
            pltpu.make_async_copy(lo.at[at], halo.at[at, :, :, pl.ds(SUB, 2)], sems.at[0, k]),
            pltpu.make_async_copy(hi.at[at], halo.at[at, :, :, pl.ds(2 * SUB - 2, 2)], sems.at[1, k]),
        ]

    @pl.when(step == 0)
    def _():
        def begin(k, carry):
            for copy in copies(k):
                copy.start()
            return carry

        lax.fori_loop(0, nb // count, begin, 0)

    for copy in copies(step):
        copy.wait()
    sub = lax.broadcasted_iota(jnp.int32, (SUB, LANES), 0)

    def block(k, carry):
        for x in range(nx):
            e = []
            for i in range(3):
                before, here, after = [halo[step * count + k, i, x, pl.ds(SUB + n, SUB), :] for n in (-1, 0, 1)]
                upper = jnp.where(sub == 0, here - 8.0 * after, here)
                lower = jnp.where(sub == SUB - 1, 8.0 * before - here, -here)
                e.append(jnp.where(sub < 2, upper, jnp.where(sub >= SUB - 2, lower, 0.0)))
            g = [gy[k, n, x] for n in range(3)]
            q = qe[k, x]
            if x in outer:
                q = q + fix[k, 0, outer[x]]
                g[1] = g[1] + fix[k, 1, outer[x]]
            square = (g[0] + g[0] + e[1]) * e[1]
            crossed = g[1] * e[0] + g[2] * e[2]
            q = q + square + (crossed + crossed)
            qe_out[k, x] = q
            if x == 0:
                first_out[k] = q
            if x == nx - 1:
                last_out[k] = q
            head_out[k, x : x + 1, :] = q[0:1]
            tail_out[k, x : x + 1, :] = q[SUB - 1 : SUB]
        return carry

    lax.fori_loop(0, count, block, 0)


def tile_edges(qe, gy, fix, lo, hi):
    nb, nx, _, _ = qe.shape
    step = steps_of(nb)
    outs = [(nx, SUB), (SUB,), (SUB,), (nx,), (nx,)]
    return pl.pallas_call(
        tile_edges_body,
        grid=(nb // step,),
        in_specs=[
            leading(step, nx, SUB, LANES),
            leading(step, 3, nx, SUB, LANES),
            leading(step, 2, 4, SUB, LANES),
            ANYWHERE,
            ANYWHERE,
        ],
        out_specs=[leading(step, *s, LANES) for s in outs],
        out_shape=[struct(nb, *s, LANES) for s in outs],
        scratch_shapes=[
            pltpu.VMEM((nb, 3, nx, 3 * SUB, LANES), F32),
            pltpu.SemaphoreType.DMA((2, nb // step)),
        ],
        compiler_params=pltpu.CompilerParams(vmem_limit_bytes=VMEM),
        cost_estimate=cost(4),
        name="tile_edges",
    )(qe, gy, fix, lo, hi)


def render_loop(sign, flags, start_copies, wait_copies, cells, smooth, speed, segments, tiles, bricks, thirds, mid, out):
    nb = cells.shape[0]
    step = steps_of(nb)
    lane = lax.broadcasted_iota(jnp.int32, (SUB, LANES), 1)
    sub = lax.broadcasted_iota(jnp.int32, (SUB, LANES), 0)
    zero = jnp.zeros((SUB, LANES), F32)
    layers = sum(size for _, size in segments)
    flipped = sign[0] == 1
    nj = smooth.shape[2] // SUB

    lax.fori_loop(0, nb // step, lambda k, carry: (start_copies(k), carry)[1], 0)
    for x in range(layers):
        for j in range(nj):
            for c in (0, nb + 1):
                smooth[c, x, SUB * j : SUB * (j + 1), :] = zero

    def blur(c):
        for load_at, store_at in tiles:
            slot = 0
            for first, size in segments:
                before = here = None
                for x in range(size + 2):
                    after = blurred_rows(cells.at[c, first + x], load_at)
                    if x >= 2:
                        smooth[c + 1, slot, pl.ds(store_at, SUB), :] = (before + after) + (here + here)
                        slot += 1
                    before, here = here, after

    def light(c):
        at = pl.ds(pl.multiple_of(c * LANES, LANES), LANES)
        for j in range(nj):
            state = Light()
            rows = pl.ds(SUB * j, SUB)
            for n in range(layers):
                slot = jnp.where(flipped, layers - 1 - n, n)
                if n % thirds == 0:
                    half = jnp.where(flipped, flags.shape[0] - 1 - n // thirds, n // thirds)
                    peak = peaks(flags, half, bricks[j], c, sub)
                if mid is not None and n == layers // 2:
                    state.behind([mid[k, rows, at] for k in range(3)], mid[3, rows, at])
                total = blurred_lanes(*[smooth[c + k, slot, rows, :] for k in range(3)], lane)
                state.add(total, speed[c, slot, rows, :], peak)
            alpha = 1.0 - state.left
            for k in range(3):
                out[k, rows, at] = 0.5 * (alpha + state.sums[k])
            out[3, rows, at] = state.left

    def group(k, carry):
        wait_copies(k)
        for n in range(step):
            c = k * step + n
            blur(c)
            if n == 0:
                pl.when(k > 0)(lambda: light(c - 1))
            else:
                light(c - 1)
        return carry

    lax.fori_loop(0, nb // step, group, 0)
    light(nb - 1)


def render_ends_body(sign, flags, qi, qx, lo, hi, speed_hbm, mid_hbm, out, cells, smooth, speed, mid, sems):
    nb, _, ny, _ = qx.shape
    step = steps_of(nb)

    def copies(k):
        at = pl.ds(k * step, step)
        columns = pl.ds(pl.multiple_of(k * step * LANES, LANES), step * LANES)
        pairs = [
            (lo.at[at], cells.at[at, 0]),
            (qx.at[at, pl.ds(0, 2)], cells.at[at, pl.ds(1, 2)]),
            (qi.at[at], cells.at[at, pl.ds(3, 4)]),
            (qx.at[at, pl.ds(2, 2)], cells.at[at, pl.ds(7, 2)]),
            (hi.at[at], cells.at[at, 9]),
            (speed_hbm.at[at], speed.at[at]),
            (mid_hbm.at[:, :, columns], mid.at[:, :, columns]),
        ]
        return [pltpu.make_async_copy(s, t, sems.at[n, k]) for n, (s, t) in enumerate(pairs)]

    render_loop(
        sign,
        flags,
        lambda k: [copy.start() for copy in copies(k)] and None,
        lambda k: [copy.wait() for copy in copies(k)] and None,
        cells,
        smooth,
        speed,
        [(0, 3), (5, 3)],
        [(start, start) for start in inner_starts(ny)],
        [(2 * j, 2 * j + 1) for j in range(ny // SUB)],
        3,
        mid,
        out,
    )


def render_ends(sign, flags, qi, qx, lo, hi, speed, mid):
    nb, _, ny, _ = qx.shape
    return pl.pallas_call(
        render_ends_body,
        in_specs=[SCALARS, SCALARS] + [ANYWHERE] * 6,
        out_specs=WHOLE,
        out_shape=struct(4, ny, nb * LANES),
        scratch_shapes=[
            pltpu.VMEM((nb, 10, ny, LANES), F32),
            pltpu.VMEM((nb + 2, 6, ny, LANES), F32),
            pltpu.VMEM((nb, 6, ny, LANES), F32),
            pltpu.VMEM((4, ny, nb * LANES), F32),
            pltpu.SemaphoreType.DMA((7, nb // steps_of(nb))),
        ],
        compiler_params=pltpu.CompilerParams(vmem_limit_bytes=VMEM),
        cost_estimate=cost(6),
        name="render_ends",
    )(sign, flags, qi, qx, lo, hi, speed, mid)


def render_rows_body(sign, flags, qe, lo, hi, row_lo, row_hi, speed_hbm, out, cells, smooth, speed, sems):
    nb, nx, _, _ = qe.shape
    step = steps_of(nb)

    def copies(k):
        at = pl.ds(k * step, step)
        rows = pl.ds(SUB, SUB)
        pairs = [
            (lo.at[at], cells.at[at, 0, rows]),
            (qe.at[at], cells.at[at, pl.ds(1, nx), rows]),
            (hi.at[at], cells.at[at, nx + 1, rows]),
            (row_lo.at[at], cells.at[at, :, SUB - 1]),
            (row_hi.at[at], cells.at[at, :, 2 * SUB]),
            (speed_hbm.at[at], speed.at[at]),
        ]
        return [pltpu.make_async_copy(s, t, sems.at[n, k]) for n, (s, t) in enumerate(pairs)]

    render_loop(
        sign,
        flags,
        lambda k: [copy.start() for copy in copies(k)] and None,
        lambda k: [copy.wait() for copy in copies(k)] and None,
        cells,
        smooth,
        speed,
        [(0, nx)],
        [(SUB, 0)],
        [(0, flags.shape[1] - 1)],
        8,
        None,
        out,
    )


def render_rows(sign, flags, qe, lo, hi, row_lo, row_hi, speed):
    nb, nx, _, _ = qe.shape
    return pl.pallas_call(
        render_rows_body,
        in_specs=[SCALARS, SCALARS] + [ANYWHERE] * 6,
        out_specs=WHOLE,
        out_shape=struct(4, SUB, nb * LANES),
        scratch_shapes=[
            pltpu.VMEM((nb, nx + 2, 3 * SUB, LANES), F32),
            pltpu.VMEM((nb + 2, nx, SUB, LANES), F32),
            pltpu.VMEM((nb, nx, SUB, LANES), F32),
            pltpu.SemaphoreType.DMA((6, nb // steps_of(nb))),
        ],
        compiler_params=pltpu.CompilerParams(vmem_limit_bytes=VMEM),
        cost_estimate=cost(4),
        name="render_rows",
    )(sign, flags, qe, lo, hi, row_lo, row_hi, speed)


def shifted(value, axis, step):
    count = lax.axis_size(axis)
    return lax.ppermute(value, axis, [(i, i + step) for i in range(count) if 0 <= i + step < count])


def from_partner(value, axis, bit):
    mask = 2**bit
    pairs = [(source, source ^ mask) for source in range(lax.axis_size(axis))]
    return lax.ppermute(value, axis, pairs)


def composite(partial, flipped):
    _, ny, nz = partial.shape
    depth_count = lax.axis_size("depth")
    width = nz // depth_count
    position = lax.axis_index("depth")
    current = partial.reshape(4, ny, depth_count, width)
    for bit in range(depth_count.bit_length() - 1):
        view = current.reshape(4, ny, current.shape[2] // 2, 2, width)
        is_lower = position >> bit & 1 == 0
        keep = jnp.where(is_lower, view[:, :, :, 0], view[:, :, :, 1])
        give = jnp.where(is_lower, view[:, :, :, 1], view[:, :, :, 0])
        take = from_partner(give, "depth", bit)
        front = jnp.where(is_lower != flipped, keep, take)
        back = jnp.where(is_lower != flipped, take, keep)
        current = jnp.concatenate([front[:3], jnp.zeros_like(front[3:])]) + front[3:] * back
    return current.reshape(4, ny, width)


def per_device(vel, view_sign, brick_flags):
    _, nx, ny, _ = vel.shape
    head, tail = sends(send_rows_body, vel, 3, nx, 2)
    rows_lo = shifted(tail, "tile", 1)
    rows_hi = shifted(head, "tile", -1)
    head, tail = sends(send_layers_body, vel, 3, 2, ny)
    layers_lo = shifted(tail, "depth", 1)
    layers_hi = shifted(head, "depth", -1)

    mid, qi, qx, speed_x, gx, qe, speed_e, gy = volume(view_sign, brick_flags, vel)
    qx, first, last, fix = depth_edges(qx, gx, layers_lo, layers_hi)
    q_lo = shifted(last, "depth", 1)
    q_hi = shifted(first, "depth", -1)
    qe, first, last, head, tail = tile_edges(qe, gy, fix, rows_lo, rows_hi)
    e_lo = shifted(last, "depth", 1)
    e_hi = shifted(first, "depth", -1)
    tail = jnp.concatenate([e_lo[:, SUB - 1 :], tail, e_hi[:, SUB - 1 :]], axis=1)
    head = jnp.concatenate([e_lo[:, :1], head, e_hi[:, :1]], axis=1)
    row_lo = shifted(tail, "tile", 1)
    row_hi = shifted(head, "tile", -1)
    flipped = view_sign[0] == 1
    main = render_ends(view_sign, brick_flags, qi, qx, q_lo, q_hi, speed_x, mid)
    main = composite(main, flipped)
    side = render_rows(view_sign, brick_flags, qe, e_lo, e_hi, row_lo, row_hi, speed_e)
    side = composite(side, flipped)
    image = jnp.concatenate([side[:, 0:3], main[:, 3 : ny - 3], side[:, SUB - 3 :]], axis=1)
    return image[:3], 1.0 - image[3]


def solution(mesh):
    placed = (P(None, "depth", "tile", None), P("tile"), P("depth", "tile", None))
    return jax.shard_map(
        per_device,
        mesh=mesh,
        in_specs=placed,
        out_specs=(P(None, "tile", "depth"), P("tile", "depth")),
        check_vma=False,
    )
```

```python
import jax
import jax.numpy as jnp
from jax import lax
from jax.experimental import pallas as pl
from jax.experimental.pallas import tpu as pltpu
from jax.sharding import PartitionSpec as P

ALPHA_PEAK = 0.04
LANES = 128
SUB = 8
HALF = SUB // 2
VMEM = 60 << 20
F32 = jnp.float32
Q_SCALE = -0.5 / (12.0 * 12.0 * 64.0)


def struct(*shape):
    return jax.ShapeDtypeStruct(shape, F32)


def leading(*block):
    return pl.BlockSpec(block, lambda b, n=len(block): (b,) + (0,) * (n - 1))


def steps_of(blocks):
    return 4 if blocks % 4 == 0 else 1


ANYWHERE = pl.BlockSpec(memory_space=pl.ANY)
WHOLE = pl.BlockSpec(memory_space=pltpu.VMEM)
SCALARS = pl.BlockSpec(memory_space=pltpu.SMEM)


def cost(microseconds):
    size = int(microseconds * 3e6)
    return pl.CostEstimate(flops=0, bytes_accessed=size, transcendentals=0)


def diff(m2, m1, p1, p2):
    if m2 is not None and m1 is not None and p1 is not None and p2 is not None:
        return 8.0 * (p1 - m1) + (m2 - p2)
    total = None
    for value, weight in ((m2, 1.0), (m1, -8.0), (p1, 8.0), (p2, -1.0)):
        if value is not None:
            total = weight * value if total is None else total + weight * value
    return total


def send_rows_body(vel, head, tail, sems):
    ny = vel.shape[2]
    nb = head.shape[0]

    def copies(k):
        at = pl.ds(pl.multiple_of(k * LANES, LANES), LANES)
        return [
            pltpu.make_async_copy(vel.at[:, :, pl.ds(row, 2), at], to.at[k], sems.at[n, k])
            for n, (row, to) in enumerate(((0, head), (ny - 2, tail)))
        ]

    run(copies, nb)


def send_layers_body(vel, head, tail, sems):
    nx = vel.shape[1]
    nb = head.shape[0]

    def copies(k):
        at = pl.ds(pl.multiple_of(k * LANES, LANES), LANES)
        return [
            pltpu.make_async_copy(vel.at[:, pl.ds(x, 2), :, at], to.at[k], sems.at[n, k])
            for n, (x, to) in enumerate(((0, head), (nx - 2, tail)))
        ]

    run(copies, nb)


def run(copies, count):
    def begin(k, carry):
        for copy in copies(k):
            copy.start()
        return carry

    def finish(k, carry):
        for copy in copies(k):
            copy.wait()
        return carry

    lax.fori_loop(0, count, begin, 0)
    lax.fori_loop(0, count, finish, 0)


def sends(body, vel, *block):
    nb = vel.shape[3] // LANES
    return pl.pallas_call(
        body,
        in_specs=[ANYWHERE],
        out_specs=[WHOLE] * 2,
        out_shape=[struct(nb, *block, LANES)] * 2,
        scratch_shapes=[pltpu.SemaphoreType.DMA((2, nb))],
        compiler_params=pltpu.CompilerParams(vmem_limit_bytes=VMEM),
        cost_estimate=cost(3),
        name=body.__name__,
    )(vel)


def volume_body(sign, flags, vel, mid, qi, qx, speed_x, gx, qe, speed_e, gy, cells, qring, smooth, sems):
    _, nx, ny, nz = vel.shape
    nb, nj = nz // LANES, ny // SUB
    b = pl.program_id(0)

    def chunk(k):
        at = pl.ds(pl.multiple_of(k * LANES, LANES), LANES)
        return pltpu.make_async_copy(
            vel.at[:, :, :, at], cells.at[:, k + 1, :, SUB : SUB + ny, :], sems.at[k]
        )

    @pl.when(b == 0)
    def _():
        def begin(k, carry):
            chunk(k).start()
            return carry

        lax.fori_loop(0, nb, begin, 0)
        zero = jnp.zeros((SUB, LANES), F32)

        def clear_rows(k, carry):
            for i in range(3):
                for x in range(nx):
                    cells[i, k + 1, x, 0:SUB, :] = zero
                    cells[i, k + 1, x, SUB + ny : ny + 2 * SUB, :] = zero
            return carry

        lax.fori_loop(0, nb, clear_rows, 0)
        for j in range(nj):
            for x in range(nx):
                for i in range(3):
                    cells[i, 0, x, SUB * (j + 1) : SUB * (j + 2), :] = zero
                    cells[i, nb + 1, x, SUB * (j + 1) : SUB * (j + 2), :] = zero
            for x in range(nx - 6):
                smooth[0, x, SUB * j : SUB * (j + 1), :] = zero
                smooth[nb + 1, x, SUB * j : SUB * (j + 1), :] = zero
        chunk(0).wait()

    @pl.when(b + 1 < nb)
    def _():
        chunk(b + 1).wait()

    lane = lax.broadcasted_iota(jnp.int32, (SUB, LANES), 1)
    sub = lax.broadcasted_iota(jnp.int32, (SUB, LANES), 0)
    outer = {0: 0, 1: 1, nx - 2: 2, nx - 1: 3}
    inner = {2: 0, 3: 1, nx - 4: 2, nx - 3: 3}
    ends = {0: 0, 1: 1, 2: 2, nx - 3: 3, nx - 2: 4, nx - 1: 5}

    def q_stage():
        for j in range(nj):
            row = SUB * (j + 1)

            def tile(i, x, block=0, shift=0, row=row):
                return cells[i, b + 1 + block, x, pl.ds(row + shift, SUB), :]

            window = {(i, x): tile(i, x) for i in range(3) for x in range(2)}
            for x in range(nx):
                if x + 2 < nx:
                    for i in range(3):
                        window[i, x + 2] = tile(i, x + 2)
                g = []
                for i in range(3):
                    here = window[i, x]
                    left, right = tile(i, x, -1), tile(i, x, 1)
                    along_x = diff(*[window.get((i, x + k)) for k in (-2, -1, 1, 2)])
                    along_y = diff(*[tile(i, x, 0, k) for k in (-2, -1, 1, 2)])
                    along_z = diff(
                        pltpu.roll(jnp.where(lane >= LANES - 2, left, here), 2, 1),
                        pltpu.roll(jnp.where(lane >= LANES - 1, left, here), 1, 1),
                        pltpu.roll(jnp.where(lane < 1, right, here), LANES - 1, 1),
                        pltpu.roll(jnp.where(lane < 2, right, here), LANES - 2, 1),
                    )
                    g.append((along_x, along_y, along_z))
                diagonal = g[0][0] * g[0][0] + g[1][1] * g[1][1] + g[2][2] * g[2][2]
                crossed = g[0][1] * g[1][0] + g[0][2] * g[2][0] + g[1][2] * g[2][1]
                q_here = diagonal + (crossed + crossed)
                rows = pl.ds(SUB * j, SUB)
                qring[b % 2, x, rows, :] = q_here
                if x in outer:
                    qx[0, outer[x], rows, :] = q_here
                    for k in range(3):
                        gx[0, k, outer[x], rows, :] = g[0][k]
                if x in inner:
                    qi[0, inner[x], rows, :] = q_here
                if x in ends or j in (0, nj - 1):
                    speed_here = speed_term([window[i, x] for i in range(3)])
                if x in ends:
                    speed_x[0, ends[x], rows, :] = speed_here
                if j in (0, nj - 1):
                    for ref, value in (
                        (qe.at[0, x], q_here),
                        (speed_e.at[0, x], speed_here),
                        (gy.at[0, 0, x], g[1][1]),
                        (gy.at[0, 1, x], g[1][0]),
                        (gy.at[0, 2, x], g[1][2]),
                    ):
                        ref[...] = value if j == 0 else jnp.where(sub < HALF, ref[...], value)

    def blur_stage():
        for start in inner_starts(ny):
            before = here = None
            for x in range(2, nx - 2):
                after = blurred_rows(qring.at[(b - 1) % 2, x], start)
                if x >= 4:
                    smooth[b, x - 4, pl.ds(start, SUB), :] = (before + after) + (here + here)
                before, here = here, after

    def light_stage():
        c = b - 2
        flipped = sign[0] == 1
        for j in range(nj):
            state = Light()
            rows = pl.ds(SUB * j, SUB)
            for n in range(3, nx - 3):
                x = jnp.where(flipped, nx - 1 - n, n)
                if n == 3 or n % 8 == 0:
                    peak = peaks(flags, x // 8, (2 * j, 2 * j + 1), c, sub)
                total = blurred_lanes(*[smooth[c + k, x - 3, rows, :] for k in range(3)], lane)
                speed = speed_term([cells[i, c + 1, x, pl.ds(SUB * (j + 1), SUB), :] for i in range(3)])
                state.add(total, speed, peak)
            for k, value in enumerate(state.sums + [state.left]):
                mid[k, rows, :] = value

    @pl.when((b >= 1) & (b <= nb))
    def _():
        blur_stage()

    @pl.when(b >= 2)
    def _():
        light_stage()

    @pl.when(b < nb)
    def _():
        q_stage()


def inner_starts(ny):
    return [1 + SUB * k for k in range(ny // SUB - 1)] + [ny - SUB - 1]


def blurred_rows(ref, start):
    up, mid, down = [ref[pl.ds(start + k, SUB), :] for k in (-1, 0, 1)]
    return (up + down) + (mid + mid)


def blurred_lanes(left, mid, right, lane):
    left = pltpu.roll(jnp.where(lane >= LANES - 1, left, mid), 1, 1)
    right = pltpu.roll(jnp.where(lane < 1, right, mid), LANES - 1, 1)
    return (left + right) + (mid + mid)


def speed_term(u):
    return jnp.tanh(0.5 * (u[0] * u[0] + u[1] * u[1] + u[2] * u[2]) - 1.5)


def peaks(flags, x, rows, column, sub):
    upper, lower = [flags[x, row, column].astype(F32) for row in rows]
    return (0.5 * ALPHA_PEAK) * jnp.where(sub < HALF, upper, lower)


class Light:
    def __init__(self):
        self.left = jnp.ones((SUB, LANES), F32)
        self.sums = [jnp.zeros((SUB, LANES), F32) for _ in range(3)]

    def add(self, total, speed, peak):
        steep = jnp.tanh(Q_SCALE * total)
        weight = self.left * (peak + peak * steep)
        self.left = self.left - weight
        terms = (jnp.tanh((0.5 * Q_SCALE) * total), speed, -steep)
        self.sums = [s + weight * t for s, t in zip(self.sums, terms)]

    def behind(self, sums, left):
        self.sums = [s + self.left * t for s, t in zip(self.sums, sums)]
        self.left = self.left * left


def volume(sign, flags, vel):
    _, nx, ny, nz = vel.shape
    nb = nz // LANES
    shapes = [(4, ny), (4, ny), (6, ny), (3, 4, ny), (nx, SUB), (nx, SUB), (3, nx, SUB)]

    def spec(s):
        block = (1, *s, LANES)
        return pl.BlockSpec(block, lambda b, n=len(block): (jnp.minimum(b, nb - 1),) + (0,) * (n - 1))

    return pl.pallas_call(
        volume_body,
        grid=(nb + 2,),
        in_specs=[SCALARS, SCALARS, ANYWHERE],
        out_specs=[pl.BlockSpec((4, ny, LANES), lambda b: (0, 0, jnp.clip(b - 2, 0, nb - 1)))]
        + [spec(s) for s in shapes],
        out_shape=[struct(4, ny, nz)] + [struct(nb, *s, LANES) for s in shapes],
        scratch_shapes=[
            pltpu.VMEM((3, nb + 2, nx, ny + 2 * SUB, LANES), F32),
            pltpu.VMEM((2, nx, ny, LANES), F32),
            pltpu.VMEM((nb + 2, nx - 6, ny, LANES), F32),
            pltpu.SemaphoreType.DMA((nb,)),
        ],
        compiler_params=pltpu.CompilerParams(vmem_limit_bytes=VMEM),
        cost_estimate=cost(20),
        name="volume",
    )(sign, flags, vel)


def depth_edges_body(qx, gx, lo, hi, qx_out, first_out, last_out, fix_out):
    count, _, ny, _ = qx.shape
    sub = lax.broadcasted_iota(jnp.int32, (SUB, LANES), 0)

    def block(k, carry):
        for e in range(4):
            for j in range(ny // SUB):
                rows = pl.ds(SUB * j, SUB)
                d = []
                for i in range(3):
                    near = [(lo if e < 2 else hi)[k, i, n, rows, :] for n in range(2)]
                    d.append((near[0] - 8.0 * near[1], near[1], -near[0], 8.0 * near[0] - near[1])[e])
                g = [gx[k, n, e, rows, :] for n in range(3)]
                square = (g[0] + g[0] + d[0]) * d[0]
                crossed = g[1] * d[1] + g[2] * d[2]
                change = square + (crossed + crossed)
                fixed = qx[k, e, rows, :] + change
                qx_out[k, e, rows, :] = fixed
                if e == 0:
                    first_out[k, rows, :] = fixed
                if e == 3:
                    last_out[k, rows, :] = fixed
                if j == 0:
                    first = (change, d[1])
                if j == ny // SUB - 1:
                    for n, value in enumerate((change, d[1])):
                        fix_out[k, n, e] = jnp.where(sub < HALF, first[n], value)
        return carry

    lax.fori_loop(0, count, block, 0)


def depth_edges(qx, gx, lo, hi):
    nb, _, ny, _ = qx.shape
    step = steps_of(nb)
    outs = [(4, ny), (ny,), (ny,), (2, 4, SUB)]
    return pl.pallas_call(
        depth_edges_body,
        grid=(nb // step,),
        in_specs=[
            leading(step, 4, ny, LANES),
            leading(step, 3, 4, ny, LANES),
            leading(step, 3, 2, ny, LANES),
            leading(step, 3, 2, ny, LANES),
        ],
        out_specs=[leading(step, *s, LANES) for s in outs],
        out_shape=[struct(nb, *s, LANES) for s in outs],
        compiler_params=pltpu.CompilerParams(vmem_limit_bytes=VMEM),
        cost_estimate=cost(3),
        name="depth_edges",
    )(qx, gx, lo, hi)


def tile_edges_body(qe, gy, fix, first, last, lo, hi, qe_out, first_out, last_out, head_out, tail_out, halo, sems):
    count, nx, _, _ = qe.shape
    nb, ny = lo.shape[0], first.shape[1]
    outer = {0: 0, 1: 1, nx - 2: 2, nx - 1: 3}
    step = pl.program_id(0)

    def copies(k):
        at = pl.ds(k * count, count)
        return [
            pltpu.make_async_copy(lo.at[at], halo.at[at, :, :, pl.ds(SUB, 2)], sems.at[0, k]),
            pltpu.make_async_copy(hi.at[at], halo.at[at, :, :, pl.ds(2 * SUB - 2, 2)], sems.at[1, k]),
        ]

    @pl.when(step == 0)
    def _():
        def begin(k, carry):
            for copy in copies(k):
                copy.start()
            return carry

        lax.fori_loop(0, nb // count, begin, 0)

    for copy in copies(step):
        copy.wait()
    sub = lax.broadcasted_iota(jnp.int32, (SUB, LANES), 0)

    def block(k, carry):
        for x in range(nx):
            e = []
            for i in range(3):
                before, here, after = [halo[step * count + k, i, x, pl.ds(SUB + n, SUB), :] for n in (-1, 0, 1)]
                upper = jnp.where(sub == 0, here - 8.0 * after, here)
                lower = jnp.where(sub == SUB - 1, 8.0 * before - here, -here)
                e.append(jnp.where(sub < 2, upper, jnp.where(sub >= SUB - 2, lower, 0.0)))
            g = [gy[k, n, x] for n in range(3)]
            q = qe[k, x]
            if x in outer:
                q = q + fix[k, 0, outer[x]]
                g[1] = g[1] + fix[k, 1, outer[x]]
            square = (g[0] + g[0] + e[1]) * e[1]
            crossed = g[1] * e[0] + g[2] * e[2]
            q = q + square + (crossed + crossed)
            qe_out[k, x] = q
            if x in (0, nx - 1):
                whole, whole_out = (first, first_out) if x == 0 else (last, last_out)
                head, tail = pl.ds(0, SUB), pl.ds(ny - SUB, SUB)
                whole_out[k, pl.ds(SUB, ny - 2 * SUB), :] = whole[k, pl.ds(SUB, ny - 2 * SUB), :]
                whole_out[k, head, :] = jnp.where(sub < HALF, q, whole[k, head, :])
                whole_out[k, tail, :] = jnp.where(sub < HALF, whole[k, tail, :], q)
            head_out[k, x : x + 1, :] = q[0:1]
            tail_out[k, x : x + 1, :] = q[SUB - 1 : SUB]
        return carry

    lax.fori_loop(0, count, block, 0)


def tile_edges(qe, gy, fix, first, last, lo, hi):
    nb, nx, _, _ = qe.shape
    ny = first.shape[1]
    step = steps_of(nb)
    outs = [(nx, SUB), (ny,), (ny,), (nx,), (nx,)]
    return pl.pallas_call(
        tile_edges_body,
        grid=(nb // step,),
        in_specs=[
            leading(step, nx, SUB, LANES),
            leading(step, 3, nx, SUB, LANES),
            leading(step, 2, 4, SUB, LANES),
            leading(step, ny, LANES),
            leading(step, ny, LANES),
            ANYWHERE,
            ANYWHERE,
        ],
        out_specs=[leading(step, *s, LANES) for s in outs],
        out_shape=[struct(nb, *s, LANES) for s in outs],
        scratch_shapes=[
            pltpu.VMEM((nb, 3, nx, 3 * SUB, LANES), F32),
            pltpu.SemaphoreType.DMA((2, nb // step)),
        ],
        compiler_params=pltpu.CompilerParams(vmem_limit_bytes=VMEM),
        cost_estimate=cost(4),
        name="tile_edges",
    )(qe, gy, fix, first, last, lo, hi)


def render_loop(sign, flags, start_copies, wait_copies, cells, smooth, speed, segments, tiles, bricks, thirds, mid, out):
    nb = cells.shape[0]
    step = steps_of(nb)
    lane = lax.broadcasted_iota(jnp.int32, (SUB, LANES), 1)
    sub = lax.broadcasted_iota(jnp.int32, (SUB, LANES), 0)
    zero = jnp.zeros((SUB, LANES), F32)
    layers = sum(size for _, size in segments)
    flipped = sign[0] == 1
    nj = smooth.shape[2] // SUB

    lax.fori_loop(0, nb // step, lambda k, carry: (start_copies(k), carry)[1], 0)
    for x in range(layers):
        for j in range(nj):
            for c in (0, nb + 1):
                smooth[c, x, SUB * j : SUB * (j + 1), :] = zero

    def blur(c):
        for load_at, store_at in tiles:
            slot = 0
            for first, size in segments:
                before = here = None
                for x in range(size + 2):
                    after = blurred_rows(cells.at[c, first + x], load_at)
                    if x >= 2:
                        smooth[c + 1, slot, pl.ds(store_at, SUB), :] = (before + after) + (here + here)
                        slot += 1
                    before, here = here, after

    def light(c):
        at = pl.ds(pl.multiple_of(c * LANES, LANES), LANES)
        for j in range(nj):
            state = Light()
            rows = pl.ds(SUB * j, SUB)
            for n in range(layers):
                slot = jnp.where(flipped, layers - 1 - n, n)
                if n % thirds == 0:
                    half = jnp.where(flipped, flags.shape[0] - 1 - n // thirds, n // thirds)
                    peak = peaks(flags, half, bricks[j], c, sub)
                if mid is not None and n == layers // 2:
                    state.behind([mid[k, rows, at] for k in range(3)], mid[3, rows, at])
                total = blurred_lanes(*[smooth[c + k, slot, rows, :] for k in range(3)], lane)
                state.add(total, speed[c, slot, rows, :], peak)
            alpha = 1.0 - state.left
            per = out.shape[3] // LANES
            to = pl.ds(pl.multiple_of(c % per * LANES, LANES), LANES)
            for k in range(3):
                out[c // per, k, rows, to] = 0.5 * (alpha + state.sums[k])
            out[c // per, 3, rows, to] = state.left

    def group(k, carry):
        wait_copies(k)
        for n in range(step):
            c = k * step + n
            blur(c)
            if n == 0:
                pl.when(k > 0)(lambda: light(c - 1))
            else:
                light(c - 1)
        return carry

    lax.fori_loop(0, nb // step, group, 0)
    light(nb - 1)


def render_ends_body(sign, flags, qi, qx, lo, hi, speed_hbm, mid_hbm, out, cells, smooth, speed, mid, sems):
    nb, _, ny, _ = qx.shape
    step = steps_of(nb)

    def copies(k):
        at = pl.ds(k * step, step)
        columns = pl.ds(pl.multiple_of(k * step * LANES, LANES), step * LANES)
        pairs = [
            (lo.at[at], cells.at[at, 0]),
            (qx.at[at, pl.ds(0, 2)], cells.at[at, pl.ds(1, 2)]),
            (qi.at[at], cells.at[at, pl.ds(3, 4)]),
            (qx.at[at, pl.ds(2, 2)], cells.at[at, pl.ds(7, 2)]),
            (hi.at[at], cells.at[at, 9]),
            (speed_hbm.at[at], speed.at[at]),
            (mid_hbm.at[:, :, columns], mid.at[:, :, columns]),
        ]
        return [pltpu.make_async_copy(s, t, sems.at[n, k]) for n, (s, t) in enumerate(pairs)]

    render_loop(
        sign,
        flags,
        lambda k: [copy.start() for copy in copies(k)] and None,
        lambda k: [copy.wait() for copy in copies(k)] and None,
        cells,
        smooth,
        speed,
        [(0, 3), (5, 3)],
        [(start, start) for start in inner_starts(ny)],
        [(2 * j, 2 * j + 1) for j in range(ny // SUB)],
        3,
        mid,
        out,
    )


def render_ends(pieces, sign, flags, qi, qx, lo, hi, speed, mid):
    nb, _, ny, _ = qx.shape
    return pl.pallas_call(
        render_ends_body,
        in_specs=[SCALARS, SCALARS] + [ANYWHERE] * 6,
        out_specs=WHOLE,
        out_shape=struct(pieces, 4, ny, nb * LANES // pieces),
        scratch_shapes=[
            pltpu.VMEM((nb, 10, ny, LANES), F32),
            pltpu.VMEM((nb + 2, 6, ny, LANES), F32),
            pltpu.VMEM((nb, 6, ny, LANES), F32),
            pltpu.VMEM((4, ny, nb * LANES), F32),
            pltpu.SemaphoreType.DMA((7, nb // steps_of(nb))),
        ],
        compiler_params=pltpu.CompilerParams(vmem_limit_bytes=VMEM),
        cost_estimate=cost(6),
        name="render_ends",
    )(sign, flags, qi, qx, lo, hi, speed, mid)


def render_rows_body(sign, flags, qe, lo, hi, row_lo, row_hi, speed_hbm, out, cells, smooth, speed, sems):
    nb, nx, _, _ = qe.shape
    ny = lo.shape[1]
    step = steps_of(nb)

    def copies(k):
        at = pl.ds(k * step, step)
        rows = pl.ds(SUB, SUB)
        pairs = [
            (qe.at[at], cells.at[at, pl.ds(1, nx), rows]),
            (lo.at[at, pl.ds(0, HALF)], cells.at[at, 0, pl.ds(SUB, HALF)]),
            (lo.at[at, pl.ds(ny - HALF, HALF)], cells.at[at, 0, pl.ds(SUB + HALF, HALF)]),
            (hi.at[at, pl.ds(0, HALF)], cells.at[at, nx + 1, pl.ds(SUB, HALF)]),
            (hi.at[at, pl.ds(ny - HALF, HALF)], cells.at[at, nx + 1, pl.ds(SUB + HALF, HALF)]),
            (row_lo.at[at], cells.at[at, :, SUB - 1]),
            (row_hi.at[at], cells.at[at, :, 2 * SUB]),
            (speed_hbm.at[at], speed.at[at]),
        ]
        return [pltpu.make_async_copy(s, t, sems.at[n, k]) for n, (s, t) in enumerate(pairs)]

    render_loop(
        sign,
        flags,
        lambda k: [copy.start() for copy in copies(k)] and None,
        lambda k: [copy.wait() for copy in copies(k)] and None,
        cells,
        smooth,
        speed,
        [(0, nx)],
        [(SUB, 0)],
        [(0, flags.shape[1] - 1)],
        8,
        None,
        out,
    )


def render_rows(pieces, sign, flags, qe, lo, hi, row_lo, row_hi, speed):
    nb, nx, _, _ = qe.shape
    return pl.pallas_call(
        render_rows_body,
        in_specs=[SCALARS, SCALARS] + [ANYWHERE] * 6,
        out_specs=WHOLE,
        out_shape=struct(pieces, 4, SUB, nb * LANES // pieces),
        scratch_shapes=[
            pltpu.VMEM((nb, nx + 2, 3 * SUB, LANES), F32),
            pltpu.VMEM((nb + 2, nx, SUB, LANES), F32),
            pltpu.VMEM((nb, nx, SUB, LANES), F32),
            pltpu.SemaphoreType.DMA((8, nb // steps_of(nb))),
        ],
        compiler_params=pltpu.CompilerParams(vmem_limit_bytes=VMEM),
        cost_estimate=cost(4),
        name="render_rows",
    )(sign, flags, qe, lo, hi, row_lo, row_hi, speed)


def shifted(value, axis, step):
    count = lax.axis_size(axis)
    return lax.ppermute(value, axis, [(i, i + step) for i in range(count) if 0 <= i + step < count])


def from_partner(value, axis, bit):
    mask = 2**bit
    pairs = [(source, source ^ mask) for source in range(lax.axis_size(axis))]
    return lax.ppermute(value, axis, pairs)


def composite(current, flipped):
    position = lax.axis_index("depth")
    for bit in range(lax.axis_size("depth").bit_length() - 1):
        view = current.reshape(current.shape[0] // 2, 2, *current.shape[1:])
        mine = position >> bit & 1
        keep = lax.dynamic_index_in_dim(view, mine, 1, keepdims=False)
        take = from_partner(lax.dynamic_index_in_dim(view, 1 - mine, 1, keepdims=False), "depth", bit)
        mine_front = (mine == 0) != flipped
        front = jnp.where(mine_front, keep, take)
        back = jnp.where(mine_front, take, keep)
        channel = lax.broadcasted_iota(jnp.int32, front.shape, 1)
        current = jnp.where(channel < 3, front, 0.0) + front[:, 3:] * back
    return current[0]


def per_device(vel, view_sign, brick_flags):
    _, nx, ny, _ = vel.shape
    head, tail = sends(send_layers_body, vel, 3, 2, ny)
    layers_lo = shifted(tail, "depth", 1)
    layers_hi = shifted(head, "depth", -1)
    head, tail = sends(send_rows_body, vel, 3, nx, 2)
    rows_lo = shifted(tail, "tile", 1)
    rows_hi = shifted(head, "tile", -1)

    mid, qi, qx, speed_x, gx, qe, speed_e, gy = volume(view_sign, brick_flags, vel)
    qx, first, last, fix = depth_edges(qx, gx, layers_lo, layers_hi)
    qe, first, last, head, tail = tile_edges(qe, gy, fix, first, last, rows_lo, rows_hi)
    q_lo = shifted(last, "depth", 1)
    q_hi = shifted(first, "depth", -1)
    tail = jnp.concatenate([q_lo[:, ny - 1 :], tail, q_hi[:, ny - 1 :]], axis=1)
    head = jnp.concatenate([q_lo[:, :1], head, q_hi[:, :1]], axis=1)
    row_lo = shifted(tail, "tile", 1)
    row_hi = shifted(head, "tile", -1)
    pieces = lax.axis_size("depth")
    flipped = view_sign[0] == 1
    main = render_ends(pieces, view_sign, brick_flags, qi, qx, q_lo, q_hi, speed_x, mid)
    main, row_lo, row_hi = lax.optimization_barrier((main, row_lo, row_hi))
    side = render_rows(pieces, view_sign, brick_flags, qe, q_lo, q_hi, row_lo, row_hi, speed_e)
    main = composite(main, flipped)
    side = composite(side, flipped)
    image = jnp.concatenate([side[:, 0:3], main[:, 3 : ny - 3], side[:, SUB - 3 :]], axis=1)
    return image[:3], 1.0 - image[3]


def solution(mesh):
    placed = (P(None, "depth", "tile", None), P("tile"), P("depth", "tile", None))
    return jax.shard_map(
        per_device,
        mesh=mesh,
        in_specs=placed,
        out_specs=(P(None, "tile", "depth"), P("tile", "depth")),
        check_vma=False,
    )
```

```python
import jax
import jax.numpy as jnp
from jax import lax
from jax.experimental import pallas as pl
from jax.experimental.pallas import tpu as pltpu
from jax.sharding import PartitionSpec as P

ALPHA_PEAK = 0.04
LANES = 128
SUB = 8
HALF = SUB // 2
VMEM = 60 << 20
F32 = jnp.float32
Q_SCALE = -0.5 / (12.0 * 12.0 * 64.0)


def struct(*shape):
    return jax.ShapeDtypeStruct(shape, F32)


def leading(*block):
    return pl.BlockSpec(block, lambda b, n=len(block): (b,) + (0,) * (n - 1))


def trailing(*block):
    return pl.BlockSpec(block, lambda b, n=len(block): (0,) * (n - 1) + (b,))


def steps_of(blocks):
    return 4 if blocks % 4 == 0 else 1


ANYWHERE = pl.BlockSpec(memory_space=pl.ANY)
WHOLE = pl.BlockSpec(memory_space=pltpu.VMEM)
SCALARS = pl.BlockSpec(memory_space=pltpu.SMEM)


def cost(microseconds):
    return pl.CostEstimate(flops=int(microseconds * 1e9), bytes_accessed=int(microseconds * 1e6), transcendentals=0)


def diff(m2, m1, p1, p2):
    if m2 is not None and m1 is not None and p1 is not None and p2 is not None:
        return 8.0 * (p1 - m1) + (m2 - p2)
    total = None
    for value, weight in ((m2, 1.0), (m1, -8.0), (p1, 8.0), (p2, -1.0)):
        if value is not None:
            total = weight * value if total is None else total + weight * value
    return total


def send_rows_body(vel, head, tail, sems):
    ny = vel.shape[2]
    nb = head.shape[0]

    def copies(k):
        at = pl.ds(pl.multiple_of(k * LANES, LANES), LANES)
        return [
            pltpu.make_async_copy(vel.at[:, :, pl.ds(row, 2), at], to.at[k], sems.at[n, k])
            for n, (row, to) in enumerate(((0, head), (ny - 2, tail)))
        ]

    run(copies, nb)


def send_layers_body(vel, head, tail, sems):
    nx = vel.shape[1]

    def copies(k):
        return [
            pltpu.make_async_copy(vel.at[k, pl.ds(x, 2)], to.at[k], sems.at[n, k])
            for n, (x, to) in enumerate(((0, head), (nx - 2, tail)))
        ]

    run(copies, 3)


def run(copies, count):
    def begin(k, carry):
        for copy in copies(k):
            copy.start()
        return carry

    def finish(k, carry):
        for copy in copies(k):
            copy.wait()
        return carry

    lax.fori_loop(0, count, begin, 0)
    lax.fori_loop(0, count, finish, 0)


def sends(body, vel, pieces, *block):
    return pl.pallas_call(
        body,
        in_specs=[ANYWHERE],
        out_specs=[WHOLE] * 2,
        out_shape=[struct(*block)] * 2,
        scratch_shapes=[pltpu.SemaphoreType.DMA((2, pieces))],
        compiler_params=pltpu.CompilerParams(vmem_limit_bytes=60 << 20),
        cost_estimate=cost(3),
        name=body.__name__,
    )(vel)


def volume_body(sign, flags, vel, mid, qi, qx, speed_x, gx, qe, speed_e, gy, cells, qring, smooth, sems):
    _, nx, ny, nz = vel.shape
    nb, nj = nz // LANES, ny // SUB
    b = pl.program_id(0)

    def chunk(k):
        at = pl.ds(pl.multiple_of(k * LANES, LANES), LANES)
        return pltpu.make_async_copy(
            vel.at[:, :, :, at], cells.at[:, k + 1, :, SUB : SUB + ny, :], sems.at[k]
        )

    @pl.when(b == 0)
    def _():
        def begin(k, carry):
            chunk(k).start()
            return carry

        lax.fori_loop(0, nb, begin, 0)
        zero = jnp.zeros((SUB, LANES), F32)

        def clear_rows(k, carry):
            for i in range(3):
                for x in range(nx):
                    cells[i, k + 1, x, 0:SUB, :] = zero
                    cells[i, k + 1, x, SUB + ny : ny + 2 * SUB, :] = zero
            return carry

        lax.fori_loop(0, nb, clear_rows, 0)
        for j in range(nj):
            for x in range(nx):
                for i in range(3):
                    cells[i, 0, x, SUB * (j + 1) : SUB * (j + 2), :] = zero
                    cells[i, nb + 1, x, SUB * (j + 1) : SUB * (j + 2), :] = zero
            for x in range(nx - 6):
                smooth[0, x, SUB * j : SUB * (j + 1), :] = zero
                smooth[nb + 1, x, SUB * j : SUB * (j + 1), :] = zero
        chunk(0).wait()

    @pl.when(b + 1 < nb)
    def _():
        chunk(b + 1).wait()

    lane = lax.broadcasted_iota(jnp.int32, (SUB, LANES), 1)
    sub = lax.broadcasted_iota(jnp.int32, (SUB, LANES), 0)
    outer = {0: 0, 1: 1, nx - 2: 2, nx - 1: 3}
    inner = {2: 0, 3: 1, nx - 4: 2, nx - 3: 3}
    ends = {0: 0, 1: 1, 2: 2, nx - 3: 3, nx - 2: 4, nx - 1: 5}

    def q_stage():
        for j in range(nj):
            row = SUB * (j + 1)

            def tile(i, x, block=0, shift=0, row=row):
                return cells[i, b + 1 + block, x, pl.ds(row + shift, SUB), :]

            window = {(i, x): tile(i, x) for i in range(3) for x in range(2)}
            for x in range(nx):
                if x + 2 < nx:
                    for i in range(3):
                        window[i, x + 2] = tile(i, x + 2)
                g = []
                for i in range(3):
                    here = window[i, x]
                    left, right = tile(i, x, -1), tile(i, x, 1)
                    along_x = diff(*[window.get((i, x + k)) for k in (-2, -1, 1, 2)])
                    along_y = diff(*[tile(i, x, 0, k) for k in (-2, -1, 1, 2)])
                    along_z = diff(
                        pltpu.roll(jnp.where(lane >= LANES - 2, left, here), 2, 1),
                        pltpu.roll(jnp.where(lane >= LANES - 1, left, here), 1, 1),
                        pltpu.roll(jnp.where(lane < 1, right, here), LANES - 1, 1),
                        pltpu.roll(jnp.where(lane < 2, right, here), LANES - 2, 1),
                    )
                    g.append((along_x, along_y, along_z))
                diagonal = g[0][0] * g[0][0] + g[1][1] * g[1][1] + g[2][2] * g[2][2]
                crossed = g[0][1] * g[1][0] + g[0][2] * g[2][0] + g[1][2] * g[2][1]
                q_here = diagonal + (crossed + crossed)
                rows = pl.ds(SUB * j, SUB)
                qring[b % 2, x, rows, :] = q_here
                if x in outer:
                    qx[0, outer[x], rows, :] = q_here
                    for k in range(3):
                        gx[0, k, outer[x], rows, :] = g[0][k]
                if x in inner:
                    qi[0, inner[x], rows, :] = q_here
                if x in ends or j in (0, nj - 1):
                    speed_here = speed_term([window[i, x] for i in range(3)])
                if x in ends:
                    speed_x[0, ends[x], rows, :] = speed_here
                if j in (0, nj - 1):
                    for ref, value in (
                        (qe.at[0, x], q_here),
                        (speed_e.at[0, x], speed_here),
                        (gy.at[0, 0, x], g[1][1]),
                        (gy.at[0, 1, x], g[1][0]),
                        (gy.at[0, 2, x], g[1][2]),
                    ):
                        ref[...] = value if j == 0 else jnp.where(sub < HALF, ref[...], value)

    def blur_stage():
        for start in inner_starts(ny):
            before = here = None
            for x in range(2, nx - 2):
                after = blurred_rows(qring.at[(b - 1) % 2, x], start)
                if x >= 4:
                    smooth[b, x - 4, pl.ds(start, SUB), :] = (before + after) + (here + here)
                before, here = here, after

    def light_stage():
        c = b - 2
        flipped = sign[0] == 1
        for j in range(nj):
            state = Light()
            rows = pl.ds(SUB * j, SUB)
            for n in range(3, nx - 3):
                x = jnp.where(flipped, nx - 1 - n, n)
                if n == 3 or n % 8 == 0:
                    peak = peaks(flags, x // 8, (2 * j, 2 * j + 1), c, sub)
                total = blurred_lanes(*[smooth[c + k, x - 3, rows, :] for k in range(3)], lane)
                speed = speed_term([cells[i, c + 1, x, pl.ds(SUB * (j + 1), SUB), :] for i in range(3)])
                state.add(total, speed, peak)
            for k, value in enumerate(state.sums + [state.left]):
                mid[k, rows, :] = value

    @pl.when((b >= 1) & (b <= nb))
    def _():
        blur_stage()

    @pl.when(b >= 2)
    def _():
        light_stage()

    @pl.when(b < nb)
    def _():
        q_stage()


def inner_starts(ny):
    return [1 + SUB * k for k in range(ny // SUB - 1)] + [ny - SUB - 1]


def blurred_rows(ref, start):
    up, mid, down = [ref[pl.ds(start + k, SUB), :] for k in (-1, 0, 1)]
    return (up + down) + (mid + mid)


def blurred_lanes(left, mid, right, lane):
    left = pltpu.roll(jnp.where(lane >= LANES - 1, left, mid), 1, 1)
    right = pltpu.roll(jnp.where(lane < 1, right, mid), LANES - 1, 1)
    return (left + right) + (mid + mid)


def speed_term(u):
    return jnp.tanh(0.5 * (u[0] * u[0] + u[1] * u[1] + u[2] * u[2]) - 1.5)


def peaks(flags, x, rows, column, sub):
    upper, lower = [flags[x, row, column].astype(F32) for row in rows]
    return (0.5 * ALPHA_PEAK) * jnp.where(sub < HALF, upper, lower)


def layer(total, speed, peak):
    steep = jnp.tanh(Q_SCALE * total)
    return peak + peak * steep, (jnp.tanh((0.5 * Q_SCALE) * total), speed, -steep)


class Light:
    def __init__(self):
        self.left = jnp.ones((SUB, LANES), F32)
        self.sums = [jnp.zeros((SUB, LANES), F32) for _ in range(3)]

    def add(self, total, speed, peak):
        weight, terms = layer(total, speed, peak)
        weight = self.left * weight
        self.left = self.left - weight
        self.sums = [s + weight * t for s, t in zip(self.sums, terms)]

    def behind(self, sums, left):
        self.sums = [s + self.left * t for s, t in zip(self.sums, sums)]
        self.left = self.left * left


def volume(sign, flags, vel):
    _, nx, ny, nz = vel.shape
    nb = nz // LANES
    shapes = [(4, ny), (4, ny), (6, ny), (3, 4, ny), (nx, SUB), (nx, SUB), (3, nx, SUB)]

    def spec(s):
        block = (1, *s, LANES)
        return pl.BlockSpec(block, lambda b, n=len(block): (jnp.minimum(b, nb - 1),) + (0,) * (n - 1))

    return pl.pallas_call(
        volume_body,
        grid=(nb + 2,),
        in_specs=[SCALARS, SCALARS, ANYWHERE],
        out_specs=[pl.BlockSpec((4, ny, LANES), lambda b: (0, 0, jnp.clip(b - 2, 0, nb - 1)))]
        + [spec(s) for s in shapes],
        out_shape=[struct(4, ny, nz)] + [struct(nb, *s, LANES) for s in shapes],
        scratch_shapes=[
            pltpu.VMEM((3, nb + 2, nx, ny + 2 * SUB, LANES), F32),
            pltpu.VMEM((2, nx, ny, LANES), F32),
            pltpu.VMEM((nb + 2, nx - 6, ny, LANES), F32),
            pltpu.SemaphoreType.DMA((nb,)),
        ],
        compiler_params=pltpu.CompilerParams(vmem_limit_bytes=44 << 20),
        cost_estimate=cost(60),
        name="volume",
    )(sign, flags, vel)


def depth_edges_body(qx, gx, lo, hi, qx_out, first_out, last_out, fix_out):
    count, _, ny, _ = qx.shape
    sub = lax.broadcasted_iota(jnp.int32, (SUB, LANES), 0)

    def block(k, carry):
        at = pl.ds(pl.multiple_of(k * LANES, LANES), LANES)
        for e in range(4):
            for j in range(ny // SUB):
                rows = pl.ds(SUB * j, SUB)
                d = []
                for i in range(3):
                    near = [(lo if e < 2 else hi)[i, n, rows, at] for n in range(2)]
                    d.append((near[0] - 8.0 * near[1], near[1], -near[0], 8.0 * near[0] - near[1])[e])
                g = [gx[k, n, e, rows, :] for n in range(3)]
                square = (g[0] + g[0] + d[0]) * d[0]
                crossed = g[1] * d[1] + g[2] * d[2]
                change = square + (crossed + crossed)
                fixed = qx[k, e, rows, :] + change
                qx_out[k, e, rows, :] = fixed
                if e == 0:
                    first_out[k, rows, :] = fixed
                if e == 3:
                    last_out[k, rows, :] = fixed
                if j == 0:
                    first = (change, d[1])
                if j == ny // SUB - 1:
                    for n, value in enumerate((change, d[1])):
                        fix_out[k, n, e] = jnp.where(sub < HALF, first[n], value)
        return carry

    lax.fori_loop(0, count, block, 0)


def depth_edges(qx, gx, lo, hi):
    nb, _, ny, _ = qx.shape
    step = steps_of(nb)
    outs = [(4, ny), (ny,), (ny,), (2, 4, SUB)]
    return pl.pallas_call(
        depth_edges_body,
        grid=(nb // step,),
        in_specs=[
            leading(step, 4, ny, LANES),
            leading(step, 3, 4, ny, LANES),
            trailing(3, 2, ny, step * LANES),
            trailing(3, 2, ny, step * LANES),
        ],
        out_specs=[leading(step, *s, LANES) for s in outs],
        out_shape=[struct(nb, *s, LANES) for s in outs],
        compiler_params=pltpu.CompilerParams(vmem_limit_bytes=12 << 20),
        cost_estimate=cost(3),
        name="depth_edges",
    )(qx, gx, lo, hi)


def tile_edges_body(qe, gy, fix, lo, hi, qe_out, head_out, tail_out, halo, sems):
    count, nx, _, _ = qe.shape
    nb = lo.shape[0]
    outer = {0: 0, 1: 1, nx - 2: 2, nx - 1: 3}
    step = pl.program_id(0)

    def copies(k):
        at = pl.ds(k * count, count)
        return [
            pltpu.make_async_copy(lo.at[at], halo.at[at, :, :, pl.ds(SUB, 2)], sems.at[0, k]),
            pltpu.make_async_copy(hi.at[at], halo.at[at, :, :, pl.ds(2 * SUB - 2, 2)], sems.at[1, k]),
        ]

    @pl.when(step == 0)
    def _():
        def begin(k, carry):
            for copy in copies(k):
                copy.start()
            return carry

        lax.fori_loop(0, nb // count, begin, 0)

    for copy in copies(step):
        copy.wait()
    sub = lax.broadcasted_iota(jnp.int32, (SUB, LANES), 0)

    def block(k, carry):
        for x in range(nx):
            e = []
            for i in range(3):
                before, here, after = [halo[step * count + k, i, x, pl.ds(SUB + n, SUB), :] for n in (-1, 0, 1)]
                upper = jnp.where(sub == 0, here - 8.0 * after, here)
                lower = jnp.where(sub == SUB - 1, 8.0 * before - here, -here)
                e.append(jnp.where(sub < 2, upper, jnp.where(sub >= SUB - 2, lower, 0.0)))
            g = [gy[k, n, x] for n in range(3)]
            q = qe[k, x]
            if x in outer:
                q = q + fix[k, 0, outer[x]]
                g[1] = g[1] + fix[k, 1, outer[x]]
            square = (g[0] + g[0] + e[1]) * e[1]
            crossed = g[1] * e[0] + g[2] * e[2]
            q = q + square + (crossed + crossed)
            qe_out[k, x] = q
            head_out[k, x : x + 1, :] = q[0:1]
            tail_out[k, x : x + 1, :] = q[SUB - 1 : SUB]
        return carry

    lax.fori_loop(0, count, block, 0)


def tile_edges(qe, gy, fix, lo, hi):
    nb, nx, _, _ = qe.shape
    step = steps_of(nb)
    outs = [(nx, SUB), (nx,), (nx,)]
    return pl.pallas_call(
        tile_edges_body,
        grid=(nb // step,),
        in_specs=[
            leading(step, nx, SUB, LANES),
            leading(step, 3, nx, SUB, LANES),
            leading(step, 2, 4, SUB, LANES),
            ANYWHERE,
            ANYWHERE,
        ],
        out_specs=[leading(step, *s, LANES) for s in outs],
        out_shape=[struct(nb, *s, LANES) for s in outs],
        scratch_shapes=[
            pltpu.VMEM((nb, 3, nx, 3 * SUB, LANES), F32),
            pltpu.SemaphoreType.DMA((2, nb // step)),
        ],
        compiler_params=pltpu.CompilerParams(vmem_limit_bytes=20 << 20),
        cost_estimate=cost(4),
        name="tile_edges",
    )(qe, gy, fix, lo, hi)


def render_loop(sign, flags, start_copies, wait_copies, cells, smooth, speed, segments, tiles, bricks, thirds, mid, out):
    nb = cells.shape[0]
    step = steps_of(nb)
    lane = lax.broadcasted_iota(jnp.int32, (SUB, LANES), 1)
    sub = lax.broadcasted_iota(jnp.int32, (SUB, LANES), 0)
    zero = jnp.zeros((SUB, LANES), F32)
    layers = sum(size for _, size in segments)
    flipped = sign[0] == 1
    nj = smooth.shape[2] // SUB

    lax.fori_loop(0, nb // step, lambda k, carry: (start_copies(k), carry)[1], 0)
    for x in range(layers):
        for j in range(nj):
            for c in (0, nb + 1):
                smooth[c, x, SUB * j : SUB * (j + 1), :] = zero

    def blur(c):
        for load_at, store_at in tiles:
            slot = 0
            for first, size in segments:
                before = here = None
                for x in range(size + 2):
                    after = blurred_rows(cells.at[c, first + x], load_at)
                    if x >= 2:
                        smooth[c + 1, slot, pl.ds(store_at, SUB), :] = (before + after) + (here + here)
                        slot += 1
                    before, here = here, after

    def light(c):
        at = pl.ds(pl.multiple_of(c * LANES, LANES), LANES)
        for j in range(nj):
            state = Light()
            rows = pl.ds(SUB * j, SUB)
            for n in range(layers):
                slot = jnp.where(flipped, layers - 1 - n, n)
                if n % thirds == 0:
                    half = jnp.where(flipped, flags.shape[0] - 1 - n // thirds, n // thirds)
                    peak = peaks(flags, half, bricks[j], c, sub)
                if mid is not None and n == layers // 2:
                    state.behind([mid[k, rows, at] for k in range(3)], mid[3, rows, at])
                total = blurred_lanes(*[smooth[c + k, slot, rows, :] for k in range(3)], lane)
                state.add(total, speed[c, slot, rows, :], peak)
            alpha = 1.0 - state.left
            per = out.shape[3] // LANES
            to = pl.ds(pl.multiple_of(c % per * LANES, LANES), LANES)
            for k in range(3):
                out[c // per, k, rows, to] = 0.5 * (alpha + state.sums[k])
            out[c // per, 3, rows, to] = state.left

    def group(k, carry):
        wait_copies(k)
        for n in range(step):
            c = k * step + n
            blur(c)
            if n == 0:
                pl.when(k > 0)(lambda: light(c - 1))
            else:
                light(c - 1)
        return carry

    lax.fori_loop(0, nb // step, group, 0)
    light(nb - 1)


def render_ends_body(sign, flags, qi, qx, lo, hi, speed_hbm, mid_hbm, out, cells, smooth, speed, mid, sems):
    nb, _, ny, _ = qx.shape
    step = steps_of(nb)

    def copies(k):
        at = pl.ds(k * step, step)
        columns = pl.ds(pl.multiple_of(k * step * LANES, LANES), step * LANES)
        pairs = [
            (lo.at[at], cells.at[at, 0]),
            (qx.at[at, pl.ds(0, 2)], cells.at[at, pl.ds(1, 2)]),
            (qi.at[at], cells.at[at, pl.ds(3, 4)]),
            (qx.at[at, pl.ds(2, 2)], cells.at[at, pl.ds(7, 2)]),
            (hi.at[at], cells.at[at, 9]),
            (speed_hbm.at[at], speed.at[at]),
            (mid_hbm.at[:, :, columns], mid.at[:, :, columns]),
        ]
        return [pltpu.make_async_copy(s, t, sems.at[n, k]) for n, (s, t) in enumerate(pairs)]

    render_loop(
        sign,
        flags,
        lambda k: [copy.start() for copy in copies(k)] and None,
        lambda k: [copy.wait() for copy in copies(k)] and None,
        cells,
        smooth,
        speed,
        [(0, 3), (5, 3)],
        [(start, start) for start in inner_starts(ny)],
        [(2 * j, 2 * j + 1) for j in range(ny // SUB)],
        3,
        mid,
        out,
    )


def render_ends(pieces, sign, flags, qi, qx, lo, hi, speed, mid):
    nb, _, ny, _ = qx.shape
    return pl.pallas_call(
        render_ends_body,
        in_specs=[SCALARS, SCALARS] + [ANYWHERE] * 6,
        out_specs=WHOLE,
        out_shape=struct(pieces, 4, ny, nb * LANES // pieces),
        scratch_shapes=[
            pltpu.VMEM((nb, 10, ny, LANES), F32),
            pltpu.VMEM((nb + 2, 6, ny, LANES), F32),
            pltpu.VMEM((nb, 6, ny, LANES), F32),
            pltpu.VMEM((4, ny, nb * LANES), F32),
            pltpu.SemaphoreType.DMA((7, nb // steps_of(nb))),
        ],
        compiler_params=pltpu.CompilerParams(vmem_limit_bytes=20 << 20),
        cost_estimate=cost(6),
        name="render_ends",
    )(sign, flags, qi, qx, lo, hi, speed, mid)


STATE = 12


def render_rows_body(flags, place, qe, row_lo, row_hi, speed_hbm, keep, give, cells, smooth, speed, sems):
    nb, nx, _, _ = qe.shape
    step = steps_of(nb)
    lane = lax.broadcasted_iota(jnp.int32, (SUB, LANES), 1)
    sub = lax.broadcasted_iota(jnp.int32, (SUB, LANES), 0)
    bricks = (0, flags.shape[1] - 1)
    flipped = place[1] == 1

    def copies(k):
        at = pl.ds(k * step, step)
        pairs = [
            (qe.at[at], cells.at[at, :, pl.ds(SUB, SUB)]),
            (row_lo.at[at], cells.at[at, :, SUB - 1]),
            (row_hi.at[at], cells.at[at, :, 2 * SUB]),
            (speed_hbm.at[at], speed.at[at]),
        ]
        return [pltpu.make_async_copy(s, t, sems.at[n, k]) for n, (s, t) in enumerate(pairs)]

    def begin(k, carry):
        for copy in copies(k):
            copy.start()
        return carry

    lax.fori_loop(0, nb // step, begin, 0)
    zero = jnp.zeros((SUB, LANES), F32)
    for slot in range(nx + 2):
        smooth[0, slot] = zero
        smooth[nb + 1, slot] = zero

    def blur(c):
        rows = [blurred_rows(cells.at[c, x], SUB) for x in range(nx)]
        for x in range(1, nx - 1):
            smooth[c + 1, x] = (rows[x - 1] + rows[x + 1]) + (rows[x] + rows[x])
        smooth[c + 1, 0] = rows[1] + (rows[0] + rows[0])
        smooth[c + 1, nx - 1] = rows[nx - 2] + (rows[nx - 1] + rows[nx - 1])
        smooth[c + 1, nx] = rows[0]
        smooth[c + 1, nx + 1] = rows[nx - 1]

    def total(c, slot):
        return blurred_lanes(*[smooth[c + n, slot] for n in range(3)], lane)

    def light(c):
        state = Light()
        for n in range(nx - 2):
            x = jnp.where(flipped, nx - 2 - n, n + 1)
            if n == 0 or (n + 1) % 8 == 0:
                peak = peaks(flags, x // 8, bricks, c, sub)
            state.add(total(c, x), speed[c, x], peak)
        values = state.sums + [state.left]
        for end, added, brick in ((0, nx, 0), (nx - 1, nx + 1, flags.shape[0] - 1)):
            values += [total(c, end), total(c, added), speed[c, end], peaks(flags, brick, bricks, c, sub)]
        per = keep.shape[3] // LANES
        piece = c // per
        to = pl.ds(pl.multiple_of(c % per * LANES, LANES), LANES)

        mine = piece % 2 == place[0] % 2
        pl.when(mine)(lambda: put(keep, piece // 2, to, values))
        pl.when(jnp.logical_not(mine))(lambda: put(give, piece // 2, to, values))

    def group(k, carry):
        for copy in copies(k):
            copy.wait()

        def one(n, carry):
            c = k * step + n
            blur(c)
            pl.when(c > 0)(lambda: light(c - 1))
            return carry

        return lax.fori_loop(0, step, one, carry)

    lax.fori_loop(0, nb // step, group, 0)
    light(nb - 1)


def render_rows(pieces, flags, place, qe, row_lo, row_hi, speed):
    nb, nx, _, _ = qe.shape
    return pl.pallas_call(
        render_rows_body,
        in_specs=[SCALARS, SCALARS] + [ANYWHERE] * 4,
        out_specs=[WHOLE] * 2,
        out_shape=[struct(pieces // 2, STATE, SUB, nb * LANES // pieces)] * 2,
        scratch_shapes=[
            pltpu.VMEM((nb, nx, 3 * SUB, LANES), F32),
            pltpu.VMEM((nb + 2, nx + 2, SUB, LANES), F32),
            pltpu.VMEM((nb, nx, SUB, LANES), F32),
            pltpu.SemaphoreType.DMA((4, nb // steps_of(nb))),
        ],
        compiler_params=pltpu.CompilerParams(vmem_limit_bytes=20 << 20),
        cost_estimate=cost(3),
        name="render_rows",
    )(flags, place, qe, row_lo, row_hi, speed)


def join_body(bit, place, keep, take, *outs):
    pieces, width = keep.shape[0], keep.shape[3]
    is_lower = (place[0] >> bit) % 2 == 0
    flipped = place[1] == 1
    for piece in range(pieces):
        for c in range(width // LANES):
            at = pl.ds(c * LANES, LANES)
            own = [keep[piece, n, :, at] for n in range(STATE)]
            other = [take[piece, n, :, at] for n in range(STATE)]
            low = [jnp.where(is_lower, a, b) for a, b in zip(own, other)]
            high = [jnp.where(is_lower, b, a) for a, b in zip(own, other)]
            below = layer(low[8] + high[5], low[10], low[11])
            above = layer(high[4] + low[9], high[6], high[7])
            chain = [plain(low[:4]), seen(below), seen(above), plain(high[:4])]
            if len(outs) == 1:
                first, last = layer(low[4], low[6], low[7]), layer(high[8], high[10], high[11])
                chain = [seen(first)] + chain + [seen(last)]
            state = Light()
            for n, part in enumerate(chain):
                back = chain[len(chain) - 1 - n]
                part = [jnp.where(flipped, b, a) for a, b in zip(part, back)]
                state.behind(part[:3], part[3])
            if len(outs) == 1:
                alpha = 1.0 - state.left
                for n in range(3):
                    outs[0][n, :, at] = 0.5 * (alpha + state.sums[n])
                outs[0][3, :, at] = alpha
            else:
                values = state.sums + [state.left] + low[4:8] + high[8:]
                to = (piece + (place[0] >> (bit + 1))) % 2
                for index, out in enumerate(outs):
                    pl.when(to == index)(lambda: put(out, piece // 2, at, values))


def put(out, piece, at, values):
    for n, value in enumerate(values):
        out[piece, n, :, at] = value


def plain(values):
    return values


def seen(one):
    weight, terms = one
    return [weight * t for t in terms] + [1.0 - weight]


def join(bit, final, place, keep, take):
    pieces, _, _, width = keep.shape
    if final:
        outs = [struct(4, SUB, width)]
    else:
        outs = [struct(pieces // 2, STATE, SUB, width)] * 2
    return pl.pallas_call(
        lambda *refs: join_body(bit, *refs),
        in_specs=[SCALARS, WHOLE, WHOLE],
        out_specs=[WHOLE] * len(outs),
        out_shape=outs,
        compiler_params=pltpu.CompilerParams(vmem_limit_bytes=20 << 20),
        cost_estimate=cost(1),
        name="join_rows",
    )(place, keep, take)


def shifted(value, axis, step):
    count = lax.axis_size(axis)
    return lax.ppermute(value, axis, [(i, i + step) for i in range(count) if 0 <= i + step < count])


def from_partner(value, axis, bit):
    mask = 2**bit
    pairs = [(source, source ^ mask) for source in range(lax.axis_size(axis))]
    return lax.ppermute(value, axis, pairs)


def composite(current, flipped):
    position = lax.axis_index("depth")
    for bit in range(lax.axis_size("depth").bit_length() - 1):
        view = current.reshape(current.shape[0] // 2, 2, *current.shape[1:])
        mine = position >> bit & 1
        keep = lax.dynamic_index_in_dim(view, mine, 1, keepdims=False)
        take = from_partner(lax.dynamic_index_in_dim(view, 1 - mine, 1, keepdims=False), "depth", bit)
        mine_front = (mine == 0) != flipped
        front = jnp.where(mine_front, keep, take)
        back = jnp.where(mine_front, take, keep)
        channel = lax.broadcasted_iota(jnp.int32, front.shape, 1)
        current = jnp.where(channel < 3, front, 0.0) + front[:, 3:] * back
    return current[0]


def per_device(vel, view_sign, brick_flags):
    _, nx, ny, _ = vel.shape
    nb = vel.shape[3] // LANES
    head, tail = sends(send_rows_body, vel, nb, nb, 3, nx, 2, LANES)
    rows_lo = shifted(tail, "tile", 1)
    rows_hi = shifted(head, "tile", -1)
    vel_later, _, _ = lax.optimization_barrier((vel, head, tail))
    head, tail = sends(send_layers_body, vel_later, 3, 3, 2, ny, nb * LANES)
    layers_lo = shifted(tail, "depth", 1)
    layers_hi = shifted(head, "depth", -1)

    mid, qi, qx, speed_x, gx, qe, speed_e, gy = volume(view_sign, brick_flags, vel)
    qx, first, last, fix = depth_edges(qx, gx, layers_lo, layers_hi)
    qe, head, tail = tile_edges(qe, gy, fix, rows_lo, rows_hi)
    row_lo = shifted(tail, "tile", 1)
    row_hi = shifted(head, "tile", -1)
    q_lo = shifted(last, "depth", 1)
    q_hi = shifted(first, "depth", -1)

    pieces = lax.axis_size("depth")
    flipped = view_sign[0] == 1
    position = lax.axis_index("depth")
    place = jnp.stack([position, view_sign[0]])
    keep, give = render_rows(pieces, brick_flags, place, qe, row_lo, row_hi, speed_e)
    q_lo, q_hi, _ = lax.optimization_barrier((q_lo, q_hi, keep))
    main = render_ends(pieces, view_sign, brick_flags, qi, qx, q_lo, q_hi, speed_x, mid)
    main = composite(main, flipped)
    rounds = pieces.bit_length() - 1
    for bit in range(rounds):
        take = from_partner(give, "depth", bit)
        joined = join(bit, bit == rounds - 1, place, keep, take)
        if bit < rounds - 1:
            keep, give = joined
    side = joined[0]
    main = jnp.concatenate([main[:3], 1.0 - main[3:]])
    image = jnp.concatenate([side[:, 0:3], main[:, 3 : ny - 3], side[:, SUB - 3 :]], axis=1)
    return image[:3], image[3]


def solution(mesh):
    placed = (P(None, "depth", "tile", None), P("tile"), P("depth", "tile", None))
    return jax.shard_map(
        per_device,
        mesh=mesh,
        in_specs=placed,
        out_specs=(P(None, "tile", "depth"), P("tile", "depth")),
        check_vma=False,
    )
```

```python
import jax
import jax.numpy as jnp
from jax import lax
from jax.experimental import pallas as pl
from jax.experimental.pallas import tpu as pltpu
from jax.sharding import PartitionSpec as P

ALPHA_PEAK = 0.04
LANES = 128
SUB = 8
HALF = SUB // 2
VMEM = 60 << 20
F32 = jnp.float32
PRODUCTS = 2
Q_SCALE = -0.5 / (12.0 * 12.0 * 64.0)


def struct(*shape):
    return jax.ShapeDtypeStruct(shape, F32)


def leading(*block):
    return pl.BlockSpec(block, lambda b, n=len(block): (b,) + (0,) * (n - 1))


def trailing(*block):
    return pl.BlockSpec(block, lambda b, n=len(block): (0,) * (n - 1) + (b,))


def steps_of(blocks):
    return 4 if blocks % 4 == 0 else 1


ANYWHERE = pl.BlockSpec(memory_space=pl.ANY)
WHOLE = pl.BlockSpec(memory_space=pltpu.VMEM)
SCALARS = pl.BlockSpec(memory_space=pltpu.SMEM)


def cost(microseconds):
    return pl.CostEstimate(flops=int(microseconds * 1e9), bytes_accessed=int(microseconds * 1e6), transcendentals=0)


def diff(m2, m1, p1, p2):
    if m2 is not None and m1 is not None and p1 is not None and p2 is not None:
        return 8.0 * (p1 - m1) + (m2 - p2)
    total = None
    for value, weight in ((m2, 1.0), (m1, -8.0), (p1, 8.0), (p2, -1.0)):
        if value is not None:
            total = weight * value if total is None else total + weight * value
    return total


def send_rows_body(vel, head, tail, sems):
    ny = vel.shape[2]
    nb = head.shape[0]

    def copies(k):
        at = pl.ds(pl.multiple_of(k * LANES, LANES), LANES)
        return [
            pltpu.make_async_copy(vel.at[:, :, pl.ds(row, 2), at], to.at[k], sems.at[n, k])
            for n, (row, to) in enumerate(((0, head), (ny - 2, tail)))
        ]

    run(copies, nb)


def send_layers_body(vel, head, tail, sems):
    nx = vel.shape[1]

    def copies(k):
        return [
            pltpu.make_async_copy(vel.at[k, pl.ds(x, 2)], to.at[k], sems.at[n, k])
            for n, (x, to) in enumerate(((0, head), (nx - 2, tail)))
        ]

    run(copies, 3)


def run(copies, count):
    def begin(k, carry):
        for copy in copies(k):
            copy.start()
        return carry

    def finish(k, carry):
        for copy in copies(k):
            copy.wait()
        return carry

    lax.fori_loop(0, count, begin, 0)
    lax.fori_loop(0, count, finish, 0)


def sends(body, vel, pieces, *block):
    return pl.pallas_call(
        body,
        in_specs=[ANYWHERE],
        out_specs=[WHOLE] * 2,
        out_shape=[struct(*block)] * 2,
        scratch_shapes=[pltpu.SemaphoreType.DMA((2, pieces))],
        compiler_params=pltpu.CompilerParams(vmem_limit_bytes=60 << 20),
        cost_estimate=cost(3),
        name=body.__name__,
    )(vel)


def lane_weights():
    k = lax.broadcasted_iota(jnp.int32, (2 * LANES, LANES), 0)
    n = lax.broadcasted_iota(jnp.int32, (2 * LANES, LANES), 1)
    beside = k - LANES
    beside = jnp.where(beside >= LANES // 2, beside - LANES, beside + LANES)
    apart = jnp.where(k < LANES, k, beside) - n
    weight = jnp.zeros(apart.shape, F32)
    for at, value in ((-2, 1.0), (-1, -8.0), (1, 8.0), (2, -1.0)):
        weight = jnp.where(apart == at, value, weight)
    return jnp.concatenate([weight, weight]).astype(jnp.bfloat16)


def volume_body(
    sign, flags, vel, mid, qi, qx, speed_x, gx, qe, speed_e, gy, cells, halves, weights, along, qring, smooth, sems
):
    _, nx, ny, nz = vel.shape
    nb, nj = nz // LANES, ny // SUB
    step = qe.shape[0]
    first = pl.program_id(0) == 0

    def chunk(k):
        at = pl.ds(pl.multiple_of(k * LANES, LANES), LANES)
        return pltpu.make_async_copy(
            vel.at[:, :, :, at], cells.at[:, k + 1, :, SUB : SUB + ny, :], sems.at[k]
        )

    tall = 2 * SUB
    part_rows = nx * tall

    def split_stage(block):
        for i in range(PRODUCTS):
            for h in range(ny // tall):
                for x in range(nx):
                    whole = cells[i, block, x, pl.ds(SUB + tall * h, tall), :]
                    high = whole.astype(jnp.bfloat16)
                    at = pl.ds(h * part_rows + x * tall, tall)
                    halves[block, i, 0, at, :] = high
                    halves[block, i, 1, at, :] = (whole - high.astype(F32)).astype(jnp.bfloat16)

    @pl.when(first)
    def _():
        def begin(k, carry):
            chunk(k).start()
            return carry

        lax.fori_loop(0, nb, begin, 0)
        weights[...] = lane_weights()
        zero = jnp.zeros((SUB, LANES), F32)

        def clear_rows(k, carry):
            for i in range(3):
                for x in range(nx):
                    cells[i, k + 1, x, 0:SUB, :] = zero
                    cells[i, k + 1, x, SUB + ny : ny + 2 * SUB, :] = zero
            return carry

        lax.fori_loop(0, nb, clear_rows, 0)
        for j in range(nj):
            for x in range(nx):
                for i in range(3):
                    cells[i, 0, x, SUB * (j + 1) : SUB * (j + 2), :] = zero
                    cells[i, nb + 1, x, SUB * (j + 1) : SUB * (j + 2), :] = zero
                for i in range(PRODUCTS):
                    for part in range(2):
                        if j % 2 == 0:
                            none = jnp.zeros((2 * SUB, LANES), jnp.bfloat16)
                            at = pl.ds((j // 2 * nx + x) * 2 * SUB, 2 * SUB)
                            halves[0, i, part, at, :] = none
                            halves[nb + 1, i, part, at, :] = none
            for x in range(nx - 6):
                smooth[0, x, SUB * j : SUB * (j + 1), :] = zero
                smooth[nb + 1, x, SUB * j : SUB * (j + 1), :] = zero
        chunk(0).wait()
        split_stage(1)

    def one_block(k, carry):
        b = pl.program_id(0) * step + k

        def lanes_stage():
            is_left = lax.broadcasted_iota(jnp.int32, (nx * ny, LANES), 1) >= LANES // 2
            stack = []
            for i in range(PRODUCTS):
                terms = []
                for part in range(2):
                    left, here, right = [halves[b + n, i, part] for n in range(3)]
                    terms += [here, jnp.where(is_left, left, right)]
                stack.append(jnp.concatenate(terms, axis=1))
            product = jnp.dot(jnp.concatenate(stack), weights[...], preferred_element_type=F32)
            for i in range(PRODUCTS):
                along[i] = product[i * nx * ny : (i + 1) * nx * ny]

        @pl.when(b + 1 < nb)
        def _():
            chunk(b + 1).wait()
            split_stage(b + 2)

        lane = lax.broadcasted_iota(jnp.int32, (SUB, LANES), 1)
        sub = lax.broadcasted_iota(jnp.int32, (SUB, LANES), 0)
        outer = {0: 0, 1: 1, nx - 2: 2, nx - 1: 3}
        inner = {2: 0, 3: 1, nx - 4: 2, nx - 3: 3}
        ends = {0: 0, 1: 1, 2: 2, nx - 3: 3, nx - 2: 4, nx - 1: 5}

        def q_stage():
            for j in range(nj):
                if j == 0:
                    lanes_stage()
                row = SUB * (j + 1)

                def tile(i, x, block=0, shift=0, row=row):
                    return cells[i, b + 1 + block, x, pl.ds(row + shift, SUB), :]

                window = {(i, x): tile(i, x) for i in range(3) for x in range(2)}
                for x in range(nx):
                    if x + 2 < nx:
                        for i in range(3):
                            window[i, x + 2] = tile(i, x + 2)
                    g = []
                    for i in range(3):
                        along_x = diff(*[window.get((i, x + n)) for n in (-2, -1, 1, 2)])
                        along_y = diff(*[tile(i, x, 0, n) for n in (-2, -1, 1, 2)])
                        at = j // 2 * part_rows + x * tall + j % 2 * SUB
                        if i < PRODUCTS:
                            along_z = along[i, pl.ds(at, SUB), :]
                        else:
                            here = window[i, x]
                            left, right = tile(i, x, -1), tile(i, x, 1)
                            along_z = diff(
                                pltpu.roll(jnp.where(lane >= LANES - 2, left, here), 2, 1),
                                pltpu.roll(jnp.where(lane >= LANES - 1, left, here), 1, 1),
                                pltpu.roll(jnp.where(lane < 1, right, here), LANES - 1, 1),
                                pltpu.roll(jnp.where(lane < 2, right, here), LANES - 2, 1),
                            )
                        g.append((along_x, along_y, along_z))
                    diagonal = g[0][0] * g[0][0] + g[1][1] * g[1][1] + g[2][2] * g[2][2]
                    crossed = g[0][1] * g[1][0] + g[0][2] * g[2][0] + g[1][2] * g[2][1]
                    q_here = diagonal + (crossed + crossed)
                    rows = pl.ds(SUB * j, SUB)
                    qring[b % 2, x, rows, :] = q_here
                    if x in outer:
                        qx[k, outer[x], rows, :] = q_here
                        for n in range(3):
                            gx[k, n, outer[x], rows, :] = g[0][n]
                    if x in inner:
                        qi[k, inner[x], rows, :] = q_here
                    if x in ends or j in (0, nj - 1):
                        speed_here = speed_term([window[i, x] for i in range(3)])
                    if x in ends:
                        speed_x[k, ends[x], rows, :] = speed_here
                    if j in (0, nj - 1):
                        for ref, value in (
                            (qe.at[k, x], q_here),
                            (speed_e.at[k, x], speed_here),
                            (gy.at[k, 0, x], g[1][1]),
                            (gy.at[k, 1, x], g[1][0]),
                            (gy.at[k, 2, x], g[1][2]),
                        ):
                            ref[...] = value if j == 0 else jnp.where(sub < HALF, ref[...], value)

        def blur_stage():
            for start in inner_starts(ny):
                before = here = None
                for x in range(2, nx - 2):
                    after = blurred_rows(qring.at[(b - 1) % 2, x], start)
                    if x >= 4:
                        smooth[b, x - 4, pl.ds(start, SUB), :] = (before + after) + (here + here)
                    before, here = here, after

        def light_stage():
            c = b - 2
            flipped = sign[0] == 1
            for j in range(nj):
                state = Light()
                rows = pl.ds(SUB * j, SUB)
                for n in range(3, nx - 3):
                    x = jnp.where(flipped, nx - 1 - n, n)
                    if n == 3 or n % 8 == 0:
                        peak = peaks(flags, x // 8, (2 * j, 2 * j + 1), c, sub)
                    total = blurred_lanes(*[smooth[c + n, x - 3, rows, :] for n in range(3)], lane)
                    speed = speed_term([cells[i, c + 1, x, pl.ds(SUB * (j + 1), SUB), :] for i in range(3)])
                    state.add(total, speed, peak)
                for n, value in enumerate(state.sums + [state.left]):
                    mid[n, rows, pl.ds(pl.multiple_of(k * LANES, LANES), LANES)] = value

        @pl.when((b >= 1) & (b <= nb))
        def _():
            blur_stage()

        @pl.when(b >= 2)
        def _():
            light_stage()

        @pl.when(b < nb)
        def _():
            q_stage()
        return carry

    lax.fori_loop(0, step, one_block, 0)


def inner_starts(ny):
    return [1 + SUB * k for k in range(ny // SUB - 1)] + [ny - SUB - 1]


def blurred_rows(ref, start):
    up, mid, down = [ref[pl.ds(start + k, SUB), :] for k in (-1, 0, 1)]
    return (up + down) + (mid + mid)


def blurred_lanes(left, mid, right, lane):
    left = pltpu.roll(jnp.where(lane >= LANES - 1, left, mid), 1, 1)
    right = pltpu.roll(jnp.where(lane < 1, right, mid), LANES - 1, 1)
    return (left + right) + (mid + mid)


def speed_term(u):
    return jnp.tanh(0.5 * (u[0] * u[0] + u[1] * u[1] + u[2] * u[2]) - 1.5)


def peaks(flags, x, rows, column, sub):
    upper, lower = [flags[x, row, column].astype(F32) for row in rows]
    return (0.5 * ALPHA_PEAK) * jnp.where(sub < HALF, upper, lower)


def layer(total, speed, peak):
    steep = jnp.tanh(Q_SCALE * total)
    return peak + peak * steep, (jnp.tanh((0.5 * Q_SCALE) * total), speed, -steep)


class Light:
    def __init__(self):
        self.left = jnp.ones((SUB, LANES), F32)
        self.sums = [jnp.zeros((SUB, LANES), F32) for _ in range(3)]

    def add(self, total, speed, peak):
        weight, terms = layer(total, speed, peak)
        weight = self.left * weight
        self.left = self.left - weight
        self.sums = [s + weight * t for s, t in zip(self.sums, terms)]

    def behind(self, sums, left):
        self.sums = [s + self.left * t for s, t in zip(self.sums, sums)]
        self.left = self.left * left


def volume(sign, flags, vel):
    _, nx, ny, nz = vel.shape
    nb = nz // LANES
    step = 2
    shapes = [(4, ny), (4, ny), (6, ny), (3, 4, ny), (nx, SUB), (nx, SUB), (3, nx, SUB)]

    def spec(s):
        block = (step, *s, LANES)
        return pl.BlockSpec(block, lambda b, n=len(block): (jnp.minimum(b, nb // step - 1),) + (0,) * (n - 1))

    return pl.pallas_call(
        volume_body,
        grid=(nb // step + 1,),
        in_specs=[SCALARS, SCALARS, ANYWHERE],
        out_specs=[pl.BlockSpec((4, ny, step * LANES), lambda b: (0, 0, jnp.maximum(b - 1, 0)))]
        + [spec(s) for s in shapes],
        out_shape=[struct(4, ny, nz)] + [struct(nb, *s, LANES) for s in shapes],
        scratch_shapes=[
            pltpu.VMEM((3, nb + 2, nx, ny + 2 * SUB, LANES), F32),
            pltpu.VMEM((nb + 2, PRODUCTS, 2, nx * ny, LANES), jnp.bfloat16),
            pltpu.VMEM((4 * LANES, LANES), jnp.bfloat16),
            pltpu.VMEM((PRODUCTS, nx * ny, LANES), F32),
            pltpu.VMEM((2, nx, ny, LANES), F32),
            pltpu.VMEM((nb + 2, nx - 6, ny, LANES), F32),
            pltpu.SemaphoreType.DMA((nb,)),
        ],
        compiler_params=pltpu.CompilerParams(vmem_limit_bytes=40 << 20),
        cost_estimate=cost(60),
        name="volume",
    )(sign, flags, vel)


def depth_edges_body(qx, gx, lo, hi, qx_out, first_out, last_out, fix_out):
    count, _, ny, _ = qx.shape
    sub = lax.broadcasted_iota(jnp.int32, (SUB, LANES), 0)

    def block(k, carry):
        at = pl.ds(pl.multiple_of(k * LANES, LANES), LANES)
        for e in range(4):
            for j in range(ny // SUB):
                rows = pl.ds(SUB * j, SUB)
                d = []
                for i in range(3):
                    near = [(lo if e < 2 else hi)[i, n, rows, at] for n in range(2)]
                    d.append((near[0] - 8.0 * near[1], near[1], -near[0], 8.0 * near[0] - near[1])[e])
                g = [gx[k, n, e, rows, :] for n in range(3)]
                square = (g[0] + g[0] + d[0]) * d[0]
                crossed = g[1] * d[1] + g[2] * d[2]
                change = square + (crossed + crossed)
                fixed = qx[k, e, rows, :] + change
                qx_out[k, e, rows, :] = fixed
                if e == 0:
                    first_out[k, rows, :] = fixed
                if e == 3:
                    last_out[k, rows, :] = fixed
                if j == 0:
                    first = (change, d[1])
                if j == ny // SUB - 1:
                    for n, value in enumerate((change, d[1])):
                        fix_out[k, n, e] = jnp.where(sub < HALF, first[n], value)
        return carry

    lax.fori_loop(0, count, block, 0)


def depth_edges(qx, gx, lo, hi):
    nb, _, ny, _ = qx.shape
    step = steps_of(nb)
    outs = [(4, ny), (ny,), (ny,), (2, 4, SUB)]
    return pl.pallas_call(
        depth_edges_body,
        grid=(nb // step,),
        in_specs=[
            leading(step, 4, ny, LANES),
            leading(step, 3, 4, ny, LANES),
            trailing(3, 2, ny, step * LANES),
            trailing(3, 2, ny, step * LANES),
        ],
        out_specs=[leading(step, *s, LANES) for s in outs],
        out_shape=[struct(nb, *s, LANES) for s in outs],
        compiler_params=pltpu.CompilerParams(vmem_limit_bytes=6 << 20),
        cost_estimate=cost(3),
        name="depth_edges",
    )(qx, gx, lo, hi)


def tile_edges_body(qe, gy, fix, lo, hi, qe_out, head_out, tail_out, halo, sems):
    count, nx, _, _ = qe.shape
    nb = lo.shape[0]
    outer = {0: 0, 1: 1, nx - 2: 2, nx - 1: 3}
    step = pl.program_id(0)

    def copies(k):
        at = pl.ds(k * count, count)
        return [
            pltpu.make_async_copy(lo.at[at], halo.at[at, :, :, pl.ds(SUB, 2)], sems.at[0, k]),
            pltpu.make_async_copy(hi.at[at], halo.at[at, :, :, pl.ds(2 * SUB - 2, 2)], sems.at[1, k]),
        ]

    @pl.when(step == 0)
    def _():
        def begin(k, carry):
            for copy in copies(k):
                copy.start()
            return carry

        lax.fori_loop(0, nb // count, begin, 0)

    for copy in copies(step):
        copy.wait()
    sub = lax.broadcasted_iota(jnp.int32, (SUB, LANES), 0)

    def block(k, carry):
        for x in range(nx):
            e = []
            for i in range(3):
                before, here, after = [halo[step * count + k, i, x, pl.ds(SUB + n, SUB), :] for n in (-1, 0, 1)]
                upper = jnp.where(sub == 0, here - 8.0 * after, here)
                lower = jnp.where(sub == SUB - 1, 8.0 * before - here, -here)
                e.append(jnp.where(sub < 2, upper, jnp.where(sub >= SUB - 2, lower, 0.0)))
            g = [gy[k, n, x] for n in range(3)]
            q = qe[k, x]
            if x in outer:
                q = q + fix[k, 0, outer[x]]
                g[1] = g[1] + fix[k, 1, outer[x]]
            square = (g[0] + g[0] + e[1]) * e[1]
            crossed = g[1] * e[0] + g[2] * e[2]
            q = q + square + (crossed + crossed)
            qe_out[k, x] = q
            head_out[k, x : x + 1, :] = q[0:1]
            tail_out[k, x : x + 1, :] = q[SUB - 1 : SUB]
        return carry

    lax.fori_loop(0, count, block, 0)


def tile_edges(qe, gy, fix, lo, hi):
    nb, nx, _, _ = qe.shape
    step = steps_of(nb)
    outs = [(nx, SUB), (nx,), (nx,)]
    return pl.pallas_call(
        tile_edges_body,
        grid=(nb // step,),
        in_specs=[
            leading(step, nx, SUB, LANES),
            leading(step, 3, nx, SUB, LANES),
            leading(step, 2, 4, SUB, LANES),
            ANYWHERE,
            ANYWHERE,
        ],
        out_specs=[leading(step, *s, LANES) for s in outs],
        out_shape=[struct(nb, *s, LANES) for s in outs],
        scratch_shapes=[
            pltpu.VMEM((nb, 3, nx, 3 * SUB, LANES), F32),
            pltpu.SemaphoreType.DMA((2, nb // step)),
        ],
        compiler_params=pltpu.CompilerParams(vmem_limit_bytes=14 << 20),
        cost_estimate=cost(4),
        name="tile_edges",
    )(qe, gy, fix, lo, hi)


def render_loop(sign, flags, start_copies, wait_copies, cells, smooth, speed, segments, tiles, bricks, thirds, mid, out):
    nb = cells.shape[0]
    step = steps_of(nb)
    lane = lax.broadcasted_iota(jnp.int32, (SUB, LANES), 1)
    sub = lax.broadcasted_iota(jnp.int32, (SUB, LANES), 0)
    zero = jnp.zeros((SUB, LANES), F32)
    layers = sum(size for _, size in segments)
    flipped = sign[0] == 1
    nj = smooth.shape[2] // SUB

    lax.fori_loop(0, nb // step, lambda k, carry: (start_copies(k), carry)[1], 0)
    for x in range(layers):
        for j in range(nj):
            for c in (0, nb + 1):
                smooth[c, x, SUB * j : SUB * (j + 1), :] = zero

    def blur(c):
        for load_at, store_at in tiles:
            slot = 0
            for first, size in segments:
                before = here = None
                for x in range(size + 2):
                    after = blurred_rows(cells.at[c, first + x], load_at)
                    if x >= 2:
                        smooth[c + 1, slot, pl.ds(store_at, SUB), :] = (before + after) + (here + here)
                        slot += 1
                    before, here = here, after

    def light(c):
        at = pl.ds(pl.multiple_of(c * LANES, LANES), LANES)
        for j in range(nj):
            state = Light()
            rows = pl.ds(SUB * j, SUB)
            for n in range(layers):
                slot = jnp.where(flipped, layers - 1 - n, n)
                if n % thirds == 0:
                    half = jnp.where(flipped, flags.shape[0] - 1 - n // thirds, n // thirds)
                    peak = peaks(flags, half, bricks[j], c, sub)
                if mid is not None and n == layers // 2:
                    state.behind([mid[k, rows, at] for k in range(3)], mid[3, rows, at])
                total = blurred_lanes(*[smooth[c + k, slot, rows, :] for k in range(3)], lane)
                state.add(total, speed[c, slot, rows, :], peak)
            alpha = 1.0 - state.left
            per = out.shape[3] // LANES
            to = pl.ds(pl.multiple_of(c % per * LANES, LANES), LANES)
            for k in range(3):
                out[c // per, k, rows, to] = 0.5 * (alpha + state.sums[k])
            out[c // per, 3, rows, to] = state.left

    def group(k, carry):
        wait_copies(k)
        for n in range(step):
            c = k * step + n
            blur(c)
            if n == 0:
                pl.when(k > 0)(lambda: light(c - 1))
            else:
                light(c - 1)
        return carry

    lax.fori_loop(0, nb // step, group, 0)
    light(nb - 1)


def render_ends_body(sign, flags, qi, qx, lo, hi, speed_hbm, mid_hbm, out, cells, smooth, speed, mid, sems):
    nb, _, ny, _ = qx.shape
    step = steps_of(nb)

    def copies(k):
        at = pl.ds(k * step, step)
        columns = pl.ds(pl.multiple_of(k * step * LANES, LANES), step * LANES)
        pairs = [
            (lo.at[at], cells.at[at, 0]),
            (qx.at[at, pl.ds(0, 2)], cells.at[at, pl.ds(1, 2)]),
            (qi.at[at], cells.at[at, pl.ds(3, 4)]),
            (qx.at[at, pl.ds(2, 2)], cells.at[at, pl.ds(7, 2)]),
            (hi.at[at], cells.at[at, 9]),
            (speed_hbm.at[at], speed.at[at]),
            (mid_hbm.at[:, :, columns], mid.at[:, :, columns]),
        ]
        return [pltpu.make_async_copy(s, t, sems.at[n, k]) for n, (s, t) in enumerate(pairs)]

    render_loop(
        sign,
        flags,
        lambda k: [copy.start() for copy in copies(k)] and None,
        lambda k: [copy.wait() for copy in copies(k)] and None,
        cells,
        smooth,
        speed,
        [(0, 3), (5, 3)],
        [(start, start) for start in inner_starts(ny)],
        [(2 * j, 2 * j + 1) for j in range(ny // SUB)],
        3,
        mid,
        out,
    )


def render_ends(pieces, sign, flags, qi, qx, lo, hi, speed, mid):
    nb, _, ny, _ = qx.shape
    return pl.pallas_call(
        render_ends_body,
        in_specs=[SCALARS, SCALARS] + [ANYWHERE] * 6,
        out_specs=WHOLE,
        out_shape=struct(pieces, 4, ny, nb * LANES // pieces),
        scratch_shapes=[
            pltpu.VMEM((nb, 10, ny, LANES), F32),
            pltpu.VMEM((nb + 2, 6, ny, LANES), F32),
            pltpu.VMEM((nb, 6, ny, LANES), F32),
            pltpu.VMEM((4, ny, nb * LANES), F32),
            pltpu.SemaphoreType.DMA((7, nb // steps_of(nb))),
        ],
        compiler_params=pltpu.CompilerParams(vmem_limit_bytes=10 << 20),
        cost_estimate=cost(6),
        name="render_ends",
    )(sign, flags, qi, qx, lo, hi, speed, mid)


STATE = 12


def render_rows_body(flags, place, qe, row_lo, row_hi, speed_hbm, keep, give, cells, smooth, speed, sems):
    nb, nx, _, _ = qe.shape
    step = steps_of(nb)
    lane = lax.broadcasted_iota(jnp.int32, (SUB, LANES), 1)
    sub = lax.broadcasted_iota(jnp.int32, (SUB, LANES), 0)
    bricks = (0, flags.shape[1] - 1)
    flipped = place[1] == 1

    def copies(k):
        at = pl.ds(k * step, step)
        pairs = [
            (qe.at[at], cells.at[at, :, pl.ds(SUB, SUB)]),
            (row_lo.at[at], cells.at[at, :, SUB - 1]),
            (row_hi.at[at], cells.at[at, :, 2 * SUB]),
            (speed_hbm.at[at], speed.at[at]),
        ]
        return [pltpu.make_async_copy(s, t, sems.at[n, k]) for n, (s, t) in enumerate(pairs)]

    def begin(k, carry):
        for copy in copies(k):
            copy.start()
        return carry

    lax.fori_loop(0, nb // step, begin, 0)
    zero = jnp.zeros((SUB, LANES), F32)
    for slot in range(nx + 2):
        smooth[0, slot] = zero
        smooth[nb + 1, slot] = zero

    def blur(c):
        rows = [blurred_rows(cells.at[c, x], SUB) for x in range(nx)]
        for x in range(1, nx - 1):
            smooth[c + 1, x] = (rows[x - 1] + rows[x + 1]) + (rows[x] + rows[x])
        smooth[c + 1, 0] = rows[1] + (rows[0] + rows[0])
        smooth[c + 1, nx - 1] = rows[nx - 2] + (rows[nx - 1] + rows[nx - 1])
        smooth[c + 1, nx] = rows[0]
        smooth[c + 1, nx + 1] = rows[nx - 1]

    def total(c, slot):
        return blurred_lanes(*[smooth[c + n, slot] for n in range(3)], lane)

    def light(c):
        state = Light()
        for n in range(nx - 2):
            x = jnp.where(flipped, nx - 2 - n, n + 1)
            if n == 0 or (n + 1) % 8 == 0:
                peak = peaks(flags, x // 8, bricks, c, sub)
            state.add(total(c, x), speed[c, x], peak)
        values = state.sums + [state.left]
        for end, added, brick in ((0, nx, 0), (nx - 1, nx + 1, flags.shape[0] - 1)):
            values += [total(c, end), total(c, added), speed[c, end], peaks(flags, brick, bricks, c, sub)]
        per = keep.shape[3] // LANES
        piece = c // per
        to = pl.ds(pl.multiple_of(c % per * LANES, LANES), LANES)

        mine = piece % 2 == place[0] % 2
        pl.when(mine)(lambda: put(keep, piece // 2, to, values))
        pl.when(jnp.logical_not(mine))(lambda: put(give, piece // 2, to, values))

    def group(k, carry):
        for copy in copies(k):
            copy.wait()

        def one(n, carry):
            c = k * step + n
            blur(c)
            pl.when(c > 0)(lambda: light(c - 1))
            return carry

        return lax.fori_loop(0, step, one, carry)

    lax.fori_loop(0, nb // step, group, 0)
    light(nb - 1)


def render_rows(pieces, flags, place, qe, row_lo, row_hi, speed):
    nb, nx, _, _ = qe.shape
    return pl.pallas_call(
        render_rows_body,
        in_specs=[SCALARS, SCALARS] + [ANYWHERE] * 4,
        out_specs=[WHOLE] * 2,
        out_shape=[struct(pieces // 2, STATE, SUB, nb * LANES // pieces)] * 2,
        scratch_shapes=[
            pltpu.VMEM((nb, nx, 3 * SUB, LANES), F32),
            pltpu.VMEM((nb + 2, nx + 2, SUB, LANES), F32),
            pltpu.VMEM((nb, nx, SUB, LANES), F32),
            pltpu.SemaphoreType.DMA((4, nb // steps_of(nb))),
        ],
        compiler_params=pltpu.CompilerParams(vmem_limit_bytes=9 << 20),
        cost_estimate=cost(3),
        name="render_rows",
    )(flags, place, qe, row_lo, row_hi, speed)


def join_body(bit, rounds, place, keep, take, *outs):
    pieces, count, _, width = keep.shape
    final = bit == rounds - 1
    is_lower = (place[0] >> bit) % 2 == 0
    next_lower = (place[0] >> (bit + 1)) % 2 == 0
    flipped = place[1] == 1
    for piece in range(pieces):
        for c in range(width // LANES):
            at = pl.ds(c * LANES, LANES)
            own = [keep[piece, n, :, at] for n in range(count)]
            other = [take[piece, n, :, at] for n in range(count)]
            low = [jnp.where(is_lower, a, b) for a, b in zip(own, other)]
            high = [jnp.where(is_lower, b, a) for a, b in zip(own, other)]
            low_end, high_end = low[count - 4 :], high[4:8]
            below = layer(low_end[0] + high_end[1], low_end[2], low_end[3])
            above = layer(high_end[0] + low_end[1], high_end[2], high_end[3])
            chain = [low[:4], seen(below), seen(above), high[:4]]
            if bit == rounds - 2:
                clear = [jnp.zeros((SUB, LANES), F32)] * 3 + [jnp.ones((SUB, LANES), F32)]
                first, last = seen(layer(low[4], low[6], low[7])), seen(layer(high[8], high[10], high[11]))
                first = [jnp.where(next_lower, a, b) for a, b in zip(first, clear)]
                last = [jnp.where(next_lower, b, a) for a, b in zip(last, clear)]
                chain = [first] + chain + [last]
                ends = [jnp.where(next_lower, b, a) for a, b in zip(low[4:8], high[8:])]
            elif not final:
                ends = low[4:8] + high[8:]
            state = Light()
            for part, back in zip(chain, chain[::-1]):
                part = [jnp.where(flipped, b, a) for a, b in zip(part, back)]
                state.behind(part[:3], part[3])
            if final:
                alpha = 1.0 - state.left
                for n in range(3):
                    outs[0][n, :, at] = 0.5 * (alpha + state.sums[n])
                outs[0][3, :, at] = alpha
            else:
                values = state.sums + [state.left] + ends
                to = (piece + (place[0] >> (bit + 1))) % 2
                for index, out in enumerate(outs):
                    pl.when(to == index)(lambda: put(out, piece // 2, at, values))


def put(out, piece, at, values):
    for n, value in enumerate(values):
        out[piece, n, :, at] = value


def seen(one):
    weight, terms = one
    return [weight * t for t in terms] + [1.0 - weight]


def join(bit, rounds, place, keep, take):
    pieces, _, _, width = keep.shape
    if bit == rounds - 1:
        outs = [struct(4, SUB, width)]
    else:
        outs = [struct(pieces // 2, 8 if bit == rounds - 2 else STATE, SUB, width)] * 2
    return pl.pallas_call(
        lambda *refs: join_body(bit, rounds, *refs),
        in_specs=[SCALARS, WHOLE, WHOLE],
        out_specs=[WHOLE] * len(outs),
        out_shape=outs,
        compiler_params=pltpu.CompilerParams(vmem_limit_bytes=4 << 20),
        cost_estimate=cost(1),
        name="join_rows",
    )(place, keep, take)


def shifted(value, axis, step):
    count = lax.axis_size(axis)
    return lax.ppermute(value, axis, [(i, i + step) for i in range(count) if 0 <= i + step < count])


def from_partner(value, axis, bit):
    mask = 2**bit
    pairs = [(source, source ^ mask) for source in range(lax.axis_size(axis))]
    return lax.ppermute(value, axis, pairs)


def composite(current, flipped):
    position = lax.axis_index("depth")
    for bit in range(lax.axis_size("depth").bit_length() - 1):
        view = current.reshape(current.shape[0] // 2, 2, *current.shape[1:])
        mine = position >> bit & 1
        keep = lax.dynamic_index_in_dim(view, mine, 1, keepdims=False)
        take = from_partner(lax.dynamic_index_in_dim(view, 1 - mine, 1, keepdims=False), "depth", bit)
        mine_front = (mine == 0) != flipped
        front = jnp.where(mine_front, keep, take)
        back = jnp.where(mine_front, take, keep)
        channel = lax.broadcasted_iota(jnp.int32, front.shape, 1)
        current = jnp.where(channel < 3, front, 0.0) + front[:, 3:] * back
    return current[0]


def per_device(vel, view_sign, brick_flags):
    _, nx, ny, _ = vel.shape
    nb = vel.shape[3] // LANES
    head, tail = sends(send_rows_body, vel, nb, nb, 3, nx, 2, LANES)
    rows_lo = shifted(tail, "tile", 1)
    rows_hi = shifted(head, "tile", -1)
    vel_later, _, _ = lax.optimization_barrier((vel, head, tail))
    head, tail = sends(send_layers_body, vel_later, 3, 3, 2, ny, nb * LANES)
    layers_lo = shifted(tail, "depth", 1)
    layers_hi = shifted(head, "depth", -1)

    mid, qi, qx, speed_x, gx, qe, speed_e, gy = volume(view_sign, brick_flags, vel)
    qx, first, last, fix = depth_edges(qx, gx, layers_lo, layers_hi)
    qe, head, tail = tile_edges(qe, gy, fix, rows_lo, rows_hi)
    row_lo = shifted(tail, "tile", 1)
    row_hi = shifted(head, "tile", -1)
    q_lo = shifted(last, "depth", 1)
    q_hi = shifted(first, "depth", -1)

    pieces = lax.axis_size("depth")
    flipped = view_sign[0] == 1
    position = lax.axis_index("depth")
    place = jnp.stack([position, view_sign[0]])
    keep, give = render_rows(pieces, brick_flags, place, qe, row_lo, row_hi, speed_e)
    q_lo, q_hi, _ = lax.optimization_barrier((q_lo, q_hi, keep))
    main = render_ends(pieces, view_sign, brick_flags, qi, qx, q_lo, q_hi, speed_x, mid)
    main = composite(main, flipped)
    rounds = pieces.bit_length() - 1
    for bit in range(rounds):
        take = from_partner(give, "depth", bit)
        joined = join(bit, rounds, place, keep, take)
        if bit < rounds - 1:
            keep, give = joined
    side = joined[0]
    main = jnp.concatenate([main[:3], 1.0 - main[3:]])
    image = jnp.concatenate([side[:, 0:3], main[:, 3 : ny - 3], side[:, SUB - 3 :]], axis=1)
    return image[:3], image[3]


def solution(mesh):
    placed = (P(None, "depth", "tile", None), P("tile"), P("depth", "tile", None))
    return jax.shard_map(
        per_device,
        mesh=mesh,
        in_specs=placed,
        out_specs=(P(None, "tile", "depth"), P("tile", "depth")),
        check_vma=False,
    )
```

```python
import jax
import jax.numpy as jnp
from jax import lax
from jax.experimental import pallas as pl
from jax.experimental.pallas import tpu as pltpu
from jax.sharding import PartitionSpec as P

ALPHA_PEAK = 0.04
LANES = 128
SUB = 8
HALF = SUB // 2
VMEM = 60 << 20
F32 = jnp.float32
PRODUCTS = 2
Q_SCALE = -0.5 / (12.0 * 12.0 * 64.0)


def struct(*shape):
    return jax.ShapeDtypeStruct(shape, F32)


def leading(*block):
    return pl.BlockSpec(block, lambda b, n=len(block): (b,) + (0,) * (n - 1))


def trailing(*block):
    return pl.BlockSpec(block, lambda b, n=len(block): (0,) * (n - 1) + (b,))


def steps_of(blocks):
    return 4 if blocks % 4 == 0 else 1


ANYWHERE = pl.BlockSpec(memory_space=pl.ANY)
WHOLE = pl.BlockSpec(memory_space=pltpu.VMEM)
SCALARS = pl.BlockSpec(memory_space=pltpu.SMEM)


def cost(microseconds):
    return pl.CostEstimate(flops=int(microseconds * 1e9), bytes_accessed=int(microseconds * 1e6), transcendentals=0)


def diff(m2, m1, p1, p2):
    if m2 is not None and m1 is not None and p1 is not None and p2 is not None:
        return 8.0 * (p1 - m1) + (m2 - p2)
    total = None
    for value, weight in ((m2, 1.0), (m1, -8.0), (p1, 8.0), (p2, -1.0)):
        if value is not None:
            total = weight * value if total is None else total + weight * value
    return total


def send_rows_body(vel, head, tail, sems):
    ny = vel.shape[2]
    nb = head.shape[0]

    def copies(k):
        at = pl.ds(pl.multiple_of(k * LANES, LANES), LANES)
        return [
            pltpu.make_async_copy(vel.at[:, :, pl.ds(row, 2), at], to.at[k], sems.at[n, k])
            for n, (row, to) in enumerate(((0, head), (ny - 2, tail)))
        ]

    run(copies, nb)


def send_layers_body(vel, head, tail, sems):
    nx = vel.shape[1]

    def copies(k):
        return [
            pltpu.make_async_copy(vel.at[k, pl.ds(x, 2)], to.at[k], sems.at[n, k])
            for n, (x, to) in enumerate(((0, head), (nx - 2, tail)))
        ]

    run(copies, 3)


def run(copies, count):
    def begin(k, carry):
        for copy in copies(k):
            copy.start()
        return carry

    def finish(k, carry):
        for copy in copies(k):
            copy.wait()
        return carry

    lax.fori_loop(0, count, begin, 0)
    lax.fori_loop(0, count, finish, 0)


def sends(body, vel, pieces, *block):
    return pl.pallas_call(
        body,
        in_specs=[ANYWHERE],
        out_specs=[WHOLE] * 2,
        out_shape=[struct(*block)] * 2,
        scratch_shapes=[pltpu.SemaphoreType.DMA((2, pieces))],
        compiler_params=pltpu.CompilerParams(vmem_limit_bytes=60 << 20),
        cost_estimate=cost(3),
        name=body.__name__,
    )(vel)


def lane_weights():
    k = lax.broadcasted_iota(jnp.int32, (2 * LANES, LANES), 0)
    n = lax.broadcasted_iota(jnp.int32, (2 * LANES, LANES), 1)
    beside = k - LANES
    beside = jnp.where(beside >= LANES // 2, beside - LANES, beside + LANES)
    apart = jnp.where(k < LANES, k, beside) - n
    weight = jnp.zeros(apart.shape, F32)
    for at, value in ((-2, 1.0), (-1, -8.0), (1, 8.0), (2, -1.0)):
        weight = jnp.where(apart == at, value, weight)
    return jnp.concatenate([weight, weight]).astype(jnp.bfloat16)


def volume_body(
    sign, flags, vel, mid, qi, qx, speed_x, gx, qe, speed_e, gy, cells, halves, weights, along, qring, smooth, sems
):
    _, nx, ny, nz = vel.shape
    nb, nj = nz // LANES, ny // SUB
    step = qe.shape[0]
    first = pl.program_id(0) == 0

    def chunk(k):
        at = pl.ds(pl.multiple_of(k * LANES, LANES), LANES)
        return pltpu.make_async_copy(
            vel.at[:, :, :, at], cells.at[:, k + 1, :, SUB : SUB + ny, :], sems.at[k]
        )

    tall = 2 * SUB
    part_rows = nx * tall

    def split_stage(block):
        for i in range(PRODUCTS):
            for h in range(ny // tall):
                for x in range(nx):
                    whole = cells[i, block, x, pl.ds(SUB + tall * h, tall), :]
                    high = whole.astype(jnp.bfloat16)
                    at = pl.ds(h * part_rows + x * tall, tall)
                    halves[block, i, 0, at, :] = high
                    halves[block, i, 1, at, :] = (whole - high.astype(F32)).astype(jnp.bfloat16)

    @pl.when(first)
    def _():
        def begin(k, carry):
            chunk(k).start()
            return carry

        lax.fori_loop(0, nb, begin, 0)
        weights[...] = lane_weights()
        zero = jnp.zeros((SUB, LANES), F32)

        def clear_rows(k, carry):
            for i in range(3):
                for x in range(nx):
                    cells[i, k + 1, x, 0:SUB, :] = zero
                    cells[i, k + 1, x, SUB + ny : ny + 2 * SUB, :] = zero
            return carry

        lax.fori_loop(0, nb, clear_rows, 0)
        for j in range(nj):
            for x in range(nx):
                for i in range(3):
                    cells[i, 0, x, SUB * (j + 1) : SUB * (j + 2), :] = zero
                    cells[i, nb + 1, x, SUB * (j + 1) : SUB * (j + 2), :] = zero
                for i in range(PRODUCTS):
                    for part in range(2):
                        if j % 2 == 0:
                            none = jnp.zeros((2 * SUB, LANES), jnp.bfloat16)
                            at = pl.ds((j // 2 * nx + x) * 2 * SUB, 2 * SUB)
                            halves[0, i, part, at, :] = none
                            halves[nb + 1, i, part, at, :] = none
            for x in range(nx - 6):
                smooth[0, x, SUB * j : SUB * (j + 1), :] = zero
                smooth[nb + 1, x, SUB * j : SUB * (j + 1), :] = zero
        chunk(0).wait()
        split_stage(1)

    def one_block(k, carry):
        b = pl.program_id(0) * step + k

        def lanes_stage():
            is_left = lax.broadcasted_iota(jnp.int32, (nx * ny, LANES), 1) >= LANES // 2
            stack = []
            for i in range(PRODUCTS):
                terms = []
                for part in range(2):
                    left, here, right = [halves[b + n, i, part] for n in range(3)]
                    terms += [here, jnp.where(is_left, left, right)]
                stack.append(jnp.concatenate(terms, axis=1))
            product = jnp.dot(jnp.concatenate(stack), weights[...], preferred_element_type=F32)
            for i in range(PRODUCTS):
                along[i] = product[i * nx * ny : (i + 1) * nx * ny]

        @pl.when(b + 1 < nb)
        def _():
            chunk(b + 1).wait()
            split_stage(b + 2)

        lane = lax.broadcasted_iota(jnp.int32, (SUB, LANES), 1)
        sub = lax.broadcasted_iota(jnp.int32, (SUB, LANES), 0)
        outer = {0: 0, 1: 1, nx - 2: 2, nx - 1: 3}
        inner = {2: 0, 3: 1, nx - 4: 2, nx - 3: 3}
        ends = {0: 0, 1: 1, 2: 2, nx - 3: 3, nx - 2: 4, nx - 1: 5}

        def q_stage():
            for j in range(nj):
                if j == 0:
                    lanes_stage()
                row = SUB * (j + 1)

                def tile(i, x, block=0, shift=0, row=row):
                    return cells[i, b + 1 + block, x, pl.ds(row + shift, SUB), :]

                window = {(i, x): tile(i, x) for i in range(3) for x in range(2)}
                for x in range(nx):
                    if x + 2 < nx:
                        for i in range(3):
                            window[i, x + 2] = tile(i, x + 2)
                    g = []
                    for i in range(3):
                        along_x = diff(*[window.get((i, x + n)) for n in (-2, -1, 1, 2)])
                        along_y = diff(*[tile(i, x, 0, n) for n in (-2, -1, 1, 2)])
                        at = j // 2 * part_rows + x * tall + j % 2 * SUB
                        if i < PRODUCTS:
                            along_z = along[i, pl.ds(at, SUB), :]
                        else:
                            here = window[i, x]
                            left, right = tile(i, x, -1), tile(i, x, 1)
                            along_z = diff(
                                pltpu.roll(jnp.where(lane >= LANES - 2, left, here), 2, 1),
                                pltpu.roll(jnp.where(lane >= LANES - 1, left, here), 1, 1),
                                pltpu.roll(jnp.where(lane < 1, right, here), LANES - 1, 1),
                                pltpu.roll(jnp.where(lane < 2, right, here), LANES - 2, 1),
                            )
                        g.append((along_x, along_y, along_z))
                    diagonal = g[0][0] * g[0][0] + g[1][1] * g[1][1] + g[2][2] * g[2][2]
                    crossed = g[0][1] * g[1][0] + g[0][2] * g[2][0] + g[1][2] * g[2][1]
                    q_here = diagonal + (crossed + crossed)
                    rows = pl.ds(SUB * j, SUB)
                    qring[b % 2, x, rows, :] = q_here
                    if x in outer:
                        qx[k, outer[x], rows, :] = q_here
                        for n in range(3):
                            gx[k, n, outer[x], rows, :] = g[0][n]
                    if x in inner:
                        qi[k, inner[x], rows, :] = q_here
                    if x in ends or j in (0, nj - 1):
                        speed_here = speed_term([window[i, x] for i in range(3)])
                    if x in ends:
                        speed_x[k, ends[x], rows, :] = speed_here
                    if j in (0, nj - 1):
                        for ref, value in (
                            (qe.at[k, x], q_here),
                            (speed_e.at[k, x], speed_here),
                            (gy.at[k, 0, x], g[1][1]),
                            (gy.at[k, 1, x], g[1][0]),
                            (gy.at[k, 2, x], g[1][2]),
                        ):
                            ref[...] = value if j == 0 else jnp.where(sub < HALF, ref[...], value)

        def blur_stage():
            for start in inner_starts(ny):
                before = here = None
                for x in range(2, nx - 2):
                    after = blurred_rows(qring.at[(b - 1) % 2, x], start)
                    if x >= 4:
                        smooth[b, x - 4, pl.ds(start, SUB), :] = (before + after) + (here + here)
                    before, here = here, after

        def light_stage():
            c = b - 2
            flipped = sign[0] == 1
            for j in range(nj):
                state = Light()
                rows = pl.ds(SUB * j, SUB)
                for n in range(3, nx - 3):
                    x = jnp.where(flipped, nx - 1 - n, n)
                    if n == 3 or n % 8 == 0:
                        peak = peaks(flags, x // 8, (2 * j, 2 * j + 1), c, sub)
                    total = blurred_lanes(*[smooth[c + n, x - 3, rows, :] for n in range(3)], lane)
                    speed = speed_term([cells[i, c + 1, x, pl.ds(SUB * (j + 1), SUB), :] for i in range(3)])
                    state.add(total, speed, peak)
                for n, value in enumerate(state.sums + [state.left]):
                    mid[n, rows, pl.ds(pl.multiple_of(k * LANES, LANES), LANES)] = value

        @pl.when((b >= 1) & (b <= nb))
        def _():
            blur_stage()

        @pl.when(b >= 2)
        def _():
            light_stage()

        @pl.when(b < nb)
        def _():
            q_stage()
        return carry

    lax.fori_loop(0, step, one_block, 0)


def inner_starts(ny):
    return [1 + SUB * k for k in range(ny // SUB - 1)] + [ny - SUB - 1]


def blurred_rows(ref, start):
    up, mid, down = [ref[pl.ds(start + k, SUB), :] for k in (-1, 0, 1)]
    return (up + down) + (mid + mid)


def blurred_lanes(left, mid, right, lane):
    left = pltpu.roll(jnp.where(lane >= LANES - 1, left, mid), 1, 1)
    right = pltpu.roll(jnp.where(lane < 1, right, mid), LANES - 1, 1)
    return (left + right) + (mid + mid)


def speed_term(u):
    return jnp.tanh(0.5 * (u[0] * u[0] + u[1] * u[1] + u[2] * u[2]) - 1.5)


def peaks(flags, x, rows, column, sub):
    upper, lower = [flags[x, row, column].astype(F32) for row in rows]
    return (0.5 * ALPHA_PEAK) * jnp.where(sub < HALF, upper, lower)


def layer(total, speed, peak):
    steep = jnp.tanh(Q_SCALE * total)
    return peak + peak * steep, (jnp.tanh((0.5 * Q_SCALE) * total), speed, -steep)


class Light:
    def __init__(self):
        self.left = jnp.ones((SUB, LANES), F32)
        self.sums = [jnp.zeros((SUB, LANES), F32) for _ in range(3)]

    def add(self, total, speed, peak):
        weight, terms = layer(total, speed, peak)
        weight = self.left * weight
        self.left = self.left - weight
        self.sums = [s + weight * t for s, t in zip(self.sums, terms)]

    def behind(self, sums, left):
        self.sums = [s + self.left * t for s, t in zip(self.sums, sums)]
        self.left = self.left * left


def volume(sign, flags, vel):
    _, nx, ny, nz = vel.shape
    nb = nz // LANES
    step = 2
    shapes = [(4, ny), (4, ny), (6, ny), (3, 4, ny), (nx, SUB), (nx, SUB), (3, nx, SUB)]

    def spec(s):
        block = (step, *s, LANES)
        return pl.BlockSpec(block, lambda b, n=len(block): (jnp.minimum(b, nb // step - 1),) + (0,) * (n - 1))

    return pl.pallas_call(
        volume_body,
        grid=(nb // step + 1,),
        in_specs=[SCALARS, SCALARS, ANYWHERE],
        out_specs=[pl.BlockSpec((4, ny, step * LANES), lambda b: (0, 0, jnp.maximum(b - 1, 0)))]
        + [spec(s) for s in shapes],
        out_shape=[struct(4, ny, nz)] + [struct(nb, *s, LANES) for s in shapes],
        scratch_shapes=[
            pltpu.VMEM((3, nb + 2, nx, ny + 2 * SUB, LANES), F32),
            pltpu.VMEM((nb + 2, PRODUCTS, 2, nx * ny, LANES), jnp.bfloat16),
            pltpu.VMEM((4 * LANES, LANES), jnp.bfloat16),
            pltpu.VMEM((PRODUCTS, nx * ny, LANES), F32),
            pltpu.VMEM((2, nx, ny, LANES), F32),
            pltpu.VMEM((nb + 2, nx - 6, ny, LANES), F32),
            pltpu.SemaphoreType.DMA((nb,)),
        ],
        compiler_params=pltpu.CompilerParams(vmem_limit_bytes=40 << 20),
        cost_estimate=cost(60),
        name="volume",
    )(sign, flags, vel)


def depth_edges_body(qx, gx, lo, hi, qx_out, first_out, last_out, fix_out):
    count, _, ny, _ = qx.shape
    sub = lax.broadcasted_iota(jnp.int32, (SUB, LANES), 0)

    def block(k, carry):
        at = pl.ds(pl.multiple_of(k * LANES, LANES), LANES)
        for e in range(4):
            for j in range(ny // SUB):
                rows = pl.ds(SUB * j, SUB)
                d = []
                for i in range(3):
                    near = [(lo if e < 2 else hi)[i, n, rows, at] for n in range(2)]
                    d.append((near[0] - 8.0 * near[1], near[1], -near[0], 8.0 * near[0] - near[1])[e])
                g = [gx[k, n, e, rows, :] for n in range(3)]
                square = (g[0] + g[0] + d[0]) * d[0]
                crossed = g[1] * d[1] + g[2] * d[2]
                change = square + (crossed + crossed)
                fixed = qx[k, e, rows, :] + change
                qx_out[k, e, rows, :] = fixed
                if e == 0:
                    first_out[k, rows, :] = fixed
                if e == 3:
                    last_out[k, rows, :] = fixed
                if j == 0:
                    first = (change, d[1])
                if j == ny // SUB - 1:
                    for n, value in enumerate((change, d[1])):
                        fix_out[k, n, e] = jnp.where(sub < HALF, first[n], value)
        return carry

    lax.fori_loop(0, count, block, 0)


def depth_edges(qx, gx, lo, hi):
    nb, _, ny, _ = qx.shape
    step = steps_of(nb)
    outs = [(4, ny), (ny,), (ny,), (2, 4, SUB)]
    return pl.pallas_call(
        depth_edges_body,
        grid=(nb // step,),
        in_specs=[
            leading(step, 4, ny, LANES),
            leading(step, 3, 4, ny, LANES),
            trailing(3, 2, ny, step * LANES),
            trailing(3, 2, ny, step * LANES),
        ],
        out_specs=[leading(step, *s, LANES) for s in outs],
        out_shape=[struct(nb, *s, LANES) for s in outs],
        compiler_params=pltpu.CompilerParams(vmem_limit_bytes=6 << 20),
        cost_estimate=cost(3),
        name="depth_edges",
    )(qx, gx, lo, hi)


def tile_edges_body(qe, gy, fix, lo, hi, qe_out, head_out, tail_out, halo, sems):
    count, nx, _, _ = qe.shape
    nb = lo.shape[0]
    outer = {0: 0, 1: 1, nx - 2: 2, nx - 1: 3}
    step = pl.program_id(0)

    def copies(k):
        at = pl.ds(k * count, count)
        return [
            pltpu.make_async_copy(lo.at[at], halo.at[at, :, :, pl.ds(SUB, 2)], sems.at[0, k]),
            pltpu.make_async_copy(hi.at[at], halo.at[at, :, :, pl.ds(2 * SUB - 2, 2)], sems.at[1, k]),
        ]

    @pl.when(step == 0)
    def _():
        def begin(k, carry):
            for copy in copies(k):
                copy.start()
            return carry

        lax.fori_loop(0, nb // count, begin, 0)

    for copy in copies(step):
        copy.wait()
    sub = lax.broadcasted_iota(jnp.int32, (SUB, LANES), 0)

    def block(k, carry):
        for x in range(nx):
            e = []
            for i in range(3):
                before, here, after = [halo[step * count + k, i, x, pl.ds(SUB + n, SUB), :] for n in (-1, 0, 1)]
                upper = jnp.where(sub == 0, here - 8.0 * after, here)
                lower = jnp.where(sub == SUB - 1, 8.0 * before - here, -here)
                e.append(jnp.where(sub < 2, upper, jnp.where(sub >= SUB - 2, lower, 0.0)))
            g = [gy[k, n, x] for n in range(3)]
            q = qe[k, x]
            if x in outer:
                q = q + fix[k, 0, outer[x]]
                g[1] = g[1] + fix[k, 1, outer[x]]
            square = (g[0] + g[0] + e[1]) * e[1]
            crossed = g[1] * e[0] + g[2] * e[2]
            q = q + square + (crossed + crossed)
            qe_out[k, x] = q
            head_out[k, x : x + 1, :] = q[0:1]
            tail_out[k, x : x + 1, :] = q[SUB - 1 : SUB]
        return carry

    lax.fori_loop(0, count, block, 0)


def tile_edges(qe, gy, fix, lo, hi):
    nb, nx, _, _ = qe.shape
    step = steps_of(nb)
    outs = [(nx, SUB), (nx,), (nx,)]
    return pl.pallas_call(
        tile_edges_body,
        grid=(nb // step,),
        in_specs=[
            leading(step, nx, SUB, LANES),
            leading(step, 3, nx, SUB, LANES),
            leading(step, 2, 4, SUB, LANES),
            ANYWHERE,
            ANYWHERE,
        ],
        out_specs=[leading(step, *s, LANES) for s in outs],
        out_shape=[struct(nb, *s, LANES) for s in outs],
        scratch_shapes=[
            pltpu.VMEM((nb, 3, nx, 3 * SUB, LANES), F32),
            pltpu.SemaphoreType.DMA((2, nb // step)),
        ],
        compiler_params=pltpu.CompilerParams(vmem_limit_bytes=14 << 20),
        cost_estimate=cost(4),
        name="tile_edges",
    )(qe, gy, fix, lo, hi)


def render_loop(sign, flags, start_copies, wait_copies, cells, smooth, speed, segments, tiles, bricks, thirds, mid, out):
    nb = cells.shape[0]
    step = steps_of(nb)
    lane = lax.broadcasted_iota(jnp.int32, (SUB, LANES), 1)
    sub = lax.broadcasted_iota(jnp.int32, (SUB, LANES), 0)
    zero = jnp.zeros((SUB, LANES), F32)
    layers = sum(size for _, size in segments)
    flipped = sign[0] == 1
    nj = smooth.shape[2] // SUB

    lax.fori_loop(0, nb // step, lambda k, carry: (start_copies(k), carry)[1], 0)
    for x in range(layers):
        for j in range(nj):
            for c in (0, nb + 1):
                smooth[c, x, SUB * j : SUB * (j + 1), :] = zero

    def blur(c):
        for load_at, store_at in tiles:
            slot = 0
            for first, size in segments:
                before = here = None
                for x in range(size + 2):
                    after = blurred_rows(cells.at[c, first + x], load_at)
                    if x >= 2:
                        smooth[c + 1, slot, pl.ds(store_at, SUB), :] = (before + after) + (here + here)
                        slot += 1
                    before, here = here, after

    def light(c):
        at = pl.ds(pl.multiple_of(c * LANES, LANES), LANES)
        for j in range(nj):
            state = Light()
            rows = pl.ds(SUB * j, SUB)
            for n in range(layers):
                slot = jnp.where(flipped, layers - 1 - n, n)
                if n % thirds == 0:
                    half = jnp.where(flipped, flags.shape[0] - 1 - n // thirds, n // thirds)
                    peak = peaks(flags, half, bricks[j], c, sub)
                if mid is not None and n == layers // 2:
                    state.behind([mid[k, rows, at] for k in range(3)], mid[3, rows, at])
                total = blurred_lanes(*[smooth[c + k, slot, rows, :] for k in range(3)], lane)
                state.add(total, speed[c, slot, rows, :], peak)
            alpha = 1.0 - state.left
            per = out.shape[3] // LANES
            to = pl.ds(pl.multiple_of(c % per * LANES, LANES), LANES)
            for k in range(3):
                out[c // per, k, rows, to] = 0.5 * (alpha + state.sums[k])
            out[c // per, 3, rows, to] = state.left

    def group(k, carry):
        wait_copies(k)
        for n in range(step):
            c = k * step + n
            blur(c)
            if n == 0:
                pl.when(k > 0)(lambda: light(c - 1))
            else:
                light(c - 1)
        return carry

    lax.fori_loop(0, nb // step, group, 0)
    light(nb - 1)


def render_ends_body(sign, flags, qi, qx, lo, hi, speed_hbm, mid_hbm, out, cells, smooth, speed, mid, sems):
    nb, _, ny, _ = qx.shape
    step = steps_of(nb)

    def copies(k):
        at = pl.ds(k * step, step)
        columns = pl.ds(pl.multiple_of(k * step * LANES, LANES), step * LANES)
        pairs = [
            (lo.at[at], cells.at[at, 0]),
            (qx.at[at, pl.ds(0, 2)], cells.at[at, pl.ds(1, 2)]),
            (qi.at[at], cells.at[at, pl.ds(3, 4)]),
            (qx.at[at, pl.ds(2, 2)], cells.at[at, pl.ds(7, 2)]),
            (hi.at[at], cells.at[at, 9]),
            (speed_hbm.at[at], speed.at[at]),
            (mid_hbm.at[:, :, columns], mid.at[:, :, columns]),
        ]
        return [pltpu.make_async_copy(s, t, sems.at[n, k]) for n, (s, t) in enumerate(pairs)]

    render_loop(
        sign,
        flags,
        lambda k: [copy.start() for copy in copies(k)] and None,
        lambda k: [copy.wait() for copy in copies(k)] and None,
        cells,
        smooth,
        speed,
        [(0, 3), (5, 3)],
        [(start, start) for start in inner_starts(ny)],
        [(2 * j, 2 * j + 1) for j in range(ny // SUB)],
        3,
        mid,
        out,
    )


def render_ends(pieces, sign, flags, qi, qx, lo, hi, speed, mid):
    nb, _, ny, _ = qx.shape
    return pl.pallas_call(
        render_ends_body,
        in_specs=[SCALARS, SCALARS] + [ANYWHERE] * 6,
        out_specs=WHOLE,
        out_shape=struct(pieces, 4, ny, nb * LANES // pieces),
        scratch_shapes=[
            pltpu.VMEM((nb, 10, ny, LANES), F32),
            pltpu.VMEM((nb + 2, 6, ny, LANES), F32),
            pltpu.VMEM((nb, 6, ny, LANES), F32),
            pltpu.VMEM((4, ny, nb * LANES), F32),
            pltpu.SemaphoreType.DMA((7, nb // steps_of(nb))),
        ],
        compiler_params=pltpu.CompilerParams(vmem_limit_bytes=10 << 20),
        cost_estimate=cost(6),
        name="render_ends",
    )(sign, flags, qi, qx, lo, hi, speed, mid)


STATE = 12


def render_rows_body(flags, place, qe, row_lo, row_hi, speed_hbm, keep, give, cells, smooth, speed, sems):
    nb, nx, _, _ = qe.shape
    step = steps_of(nb)
    lane = lax.broadcasted_iota(jnp.int32, (SUB, LANES), 1)
    sub = lax.broadcasted_iota(jnp.int32, (SUB, LANES), 0)
    bricks = (0, flags.shape[1] - 1)
    flipped = place[1] == 1

    def copies(k):
        at = pl.ds(k * step, step)
        pairs = [
            (qe.at[at], cells.at[at, :, pl.ds(SUB, SUB)]),
            (row_lo.at[at], cells.at[at, :, SUB - 1]),
            (row_hi.at[at], cells.at[at, :, 2 * SUB]),
            (speed_hbm.at[at], speed.at[at]),
        ]
        return [pltpu.make_async_copy(s, t, sems.at[n, k]) for n, (s, t) in enumerate(pairs)]

    def begin(k, carry):
        for copy in copies(k):
            copy.start()
        return carry

    lax.fori_loop(0, nb // step, begin, 0)
    zero = jnp.zeros((SUB, LANES), F32)
    for slot in range(nx + 2):
        smooth[0, slot] = zero
        smooth[nb + 1, slot] = zero

    def blur(c):
        rows = [blurred_rows(cells.at[c, x], SUB) for x in range(nx)]
        for x in range(1, nx - 1):
            smooth[c + 1, x] = (rows[x - 1] + rows[x + 1]) + (rows[x] + rows[x])
        smooth[c + 1, 0] = rows[1] + (rows[0] + rows[0])
        smooth[c + 1, nx - 1] = rows[nx - 2] + (rows[nx - 1] + rows[nx - 1])
        smooth[c + 1, nx] = rows[0]
        smooth[c + 1, nx + 1] = rows[nx - 1]

    def total(c, slot):
        return blurred_lanes(*[smooth[c + n, slot] for n in range(3)], lane)

    def light(c):
        state = Light()
        for n in range(nx - 2):
            x = jnp.where(flipped, nx - 2 - n, n + 1)
            if n == 0 or (n + 1) % 8 == 0:
                peak = peaks(flags, x // 8, bricks, c, sub)
            state.add(total(c, x), speed[c, x], peak)
        values = state.sums + [state.left]
        for end, added, brick in ((0, nx, 0), (nx - 1, nx + 1, flags.shape[0] - 1)):
            values += [total(c, end), total(c, added), speed[c, end], peaks(flags, brick, bricks, c, sub)]
        per = keep.shape[3] // LANES
        piece = c // per
        to = pl.ds(pl.multiple_of(c % per * LANES, LANES), LANES)

        mine = piece % 2 == place[0] % 2
        pl.when(mine)(lambda: put(keep, piece // 2, to, values))
        pl.when(jnp.logical_not(mine))(lambda: put(give, piece // 2, to, values))

    def group(k, carry):
        for copy in copies(k):
            copy.wait()

        def one(n, carry):
            c = k * step + n
            blur(c)
            pl.when(c > 0)(lambda: light(c - 1))
            return carry

        return lax.fori_loop(0, step, one, carry)

    lax.fori_loop(0, nb // step, group, 0)
    light(nb - 1)


def render_rows(pieces, flags, place, qe, row_lo, row_hi, speed):
    nb, nx, _, _ = qe.shape
    return pl.pallas_call(
        render_rows_body,
        in_specs=[SCALARS, SCALARS] + [ANYWHERE] * 4,
        out_specs=[WHOLE] * 2,
        out_shape=[struct(pieces // 2, STATE, SUB, nb * LANES // pieces)] * 2,
        scratch_shapes=[
            pltpu.VMEM((nb, nx, 3 * SUB, LANES), F32),
            pltpu.VMEM((nb + 2, nx + 2, SUB, LANES), F32),
            pltpu.VMEM((nb, nx, SUB, LANES), F32),
            pltpu.SemaphoreType.DMA((4, nb // steps_of(nb))),
        ],
        compiler_params=pltpu.CompilerParams(vmem_limit_bytes=9 << 20),
        cost_estimate=cost(3),
        name="render_rows",
    )(flags, place, qe, row_lo, row_hi, speed)


def join_body(bit, rounds, place, keep, take, *outs):
    pieces, count, _, width = keep.shape
    final = bit == rounds - 1
    is_lower = (place[0] >> bit) % 2 == 0
    next_lower = (place[0] >> (bit + 1)) % 2 == 0
    flipped = place[1] == 1
    for piece in range(pieces):
        for c in range(width // LANES):
            at = pl.ds(c * LANES, LANES)
            own = [keep[piece, n, :, at] for n in range(count)]
            other = [take[piece, n, :, at] for n in range(count)]
            low = [jnp.where(is_lower, a, b) for a, b in zip(own, other)]
            high = [jnp.where(is_lower, b, a) for a, b in zip(own, other)]
            low_end, high_end = low[count - 4 :], high[4:8]
            below = layer(low_end[0] + high_end[1], low_end[2], low_end[3])
            above = layer(high_end[0] + low_end[1], high_end[2], high_end[3])
            chain = [low[:4], seen(below), seen(above), high[:4]]
            if bit == rounds - 2:
                clear = [jnp.zeros((SUB, LANES), F32)] * 3 + [jnp.ones((SUB, LANES), F32)]
                first, last = seen(layer(low[4], low[6], low[7])), seen(layer(high[8], high[10], high[11]))
                first = [jnp.where(next_lower, a, b) for a, b in zip(first, clear)]
                last = [jnp.where(next_lower, b, a) for a, b in zip(last, clear)]
                chain = [first] + chain + [last]
                ends = [jnp.where(next_lower, b, a) for a, b in zip(low[4:8], high[8:])]
            elif not final:
                ends = low[4:8] + high[8:]
            state = Light()
            for part, back in zip(chain, chain[::-1]):
                part = [jnp.where(flipped, b, a) for a, b in zip(part, back)]
                state.behind(part[:3], part[3])
            if final:
                alpha = 1.0 - state.left
                for n in range(3):
                    outs[0][n, :, at] = 0.5 * (alpha + state.sums[n])
                outs[0][3, :, at] = alpha
            else:
                values = state.sums + [state.left] + ends
                to = (piece + (place[0] >> (bit + 1))) % 2
                for index, out in enumerate(outs):
                    pl.when(to == index)(lambda: put(out, piece // 2, at, values))


def put(out, piece, at, values):
    for n, value in enumerate(values):
        out[piece, n, :, at] = value


def seen(one):
    weight, terms = one
    return [weight * t for t in terms] + [1.0 - weight]


def join(bit, rounds, place, keep, take):
    pieces, _, _, width = keep.shape
    if bit == rounds - 1:
        outs = [struct(4, SUB, width)]
    else:
        outs = [struct(pieces // 2, 8 if bit == rounds - 2 else STATE, SUB, width)] * 2
    return pl.pallas_call(
        lambda *refs: join_body(bit, rounds, *refs),
        in_specs=[SCALARS, WHOLE, WHOLE],
        out_specs=[WHOLE] * len(outs),
        out_shape=outs,
        compiler_params=pltpu.CompilerParams(vmem_limit_bytes=4 << 20),
        cost_estimate=cost(1),
        name="join_rows",
    )(place, keep, take)


def shifted(value, axis, step):
    count = lax.axis_size(axis)
    return lax.ppermute(value, axis, [(i, i + step) for i in range(count) if 0 <= i + step < count])


def from_partner(value, axis, bit):
    mask = 2**bit
    pairs = [(source, source ^ mask) for source in range(lax.axis_size(axis))]
    return lax.ppermute(value, axis, pairs)


def swap(current, bit, flipped):
    view = current.reshape(current.shape[0] // 2, 2, *current.shape[1:])
    mine = lax.axis_index("depth") >> bit & 1
    keep = lax.dynamic_index_in_dim(view, mine, 1, keepdims=False)
    take = from_partner(lax.dynamic_index_in_dim(view, 1 - mine, 1, keepdims=False), "depth", bit)
    mine_front = (mine == 0) != flipped
    front = jnp.where(mine_front, keep, take)
    back = jnp.where(mine_front, take, keep)
    channel = lax.broadcasted_iota(jnp.int32, front.shape, 1)
    return jnp.where(channel < 3, front, 0.0) + front[:, 3:] * back


def per_device(vel, view_sign, brick_flags):
    _, nx, ny, _ = vel.shape
    nb = vel.shape[3] // LANES
    head, tail = sends(send_rows_body, vel, nb, nb, 3, nx, 2, LANES)
    rows_lo = shifted(tail, "tile", 1)
    rows_hi = shifted(head, "tile", -1)
    vel_later, _, _ = lax.optimization_barrier((vel, head, tail))
    head, tail = sends(send_layers_body, vel_later, 3, 3, 2, ny, nb * LANES)
    layers_lo = shifted(tail, "depth", 1)
    layers_hi = shifted(head, "depth", -1)

    mid, qi, qx, speed_x, gx, qe, speed_e, gy = volume(view_sign, brick_flags, vel)
    qx, first, last, fix = depth_edges(qx, gx, layers_lo, layers_hi)
    qe, head, tail = tile_edges(qe, gy, fix, rows_lo, rows_hi)
    row_lo = shifted(tail, "tile", 1)
    row_hi = shifted(head, "tile", -1)
    q_lo = shifted(last, "depth", 1)
    q_hi = shifted(first, "depth", -1)

    pieces = lax.axis_size("depth")
    flipped = view_sign[0] == 1
    position = lax.axis_index("depth")
    place = jnp.stack([position, view_sign[0]])
    keep, give = render_rows(pieces, brick_flags, place, qe, row_lo, row_hi, speed_e)
    q_lo, q_hi, _ = lax.optimization_barrier((q_lo, q_hi, keep))
    main = render_ends(pieces, view_sign, brick_flags, qi, qx, q_lo, q_hi, speed_x, mid)
    rounds = pieces.bit_length() - 1
    main = swap(main, 0, flipped)
    for bit in range(rounds):
        take = from_partner(give, "depth", bit)
        if bit < rounds - 1:
            main, take = lax.optimization_barrier((main, take))
            main = swap(main, bit + 1, flipped)
        joined = join(bit, rounds, place, keep, take)
        if bit < rounds - 1:
            keep, give = joined
    side = joined[0]
    main = main[0]
    main = jnp.concatenate([main[:3], 1.0 - main[3:]])
    image = jnp.concatenate([side[:, 0:3], main[:, 3 : ny - 3], side[:, SUB - 3 :]], axis=1)
    return image[:3], image[3]


def solution(mesh):
    placed = (P(None, "depth", "tile", None), P("tile"), P("depth", "tile", None))
    return jax.shard_map(
        per_device,
        mesh=mesh,
        in_specs=placed,
        out_specs=(P(None, "tile", "depth"), P("tile", "depth")),
        check_vma=False,
    )
```
